32 devices in a mesh: groups: 2 (over y), loop: 4 (over z), narrow: 2 (over x), sub: 2 (over core).
Axes of the slice: x: 2, y: 2, z: 4, core: 2. Of those that a mesh axis runs over, the one named last changes fastest.
Arguments:
- block_input_rows: bfloat16 [1024, 3072], P(('groups', 'loop'), ('narrow', 'sub')), parts along dimension 0, may hold values from -240 to 240
- frozen_up_weight: bfloat16 [3072, 12288], P(('narrow', 'sub'), 'loop'), may hold values from -0.109375 to 0.109375
- frozen_down_weight: bfloat16 [12288, 3072], P('loop', ('narrow', 'sub')), may hold values from -0.0546875 to 0.0546875
- down_first_factor: bfloat16 [12288, 64], replicated, may hold values from -0.0546875 to 0.0546875
- down_second_factor: bfloat16 [64, 3072], replicated, may hold values from -0.75 to 0.75
- modulation: float32 [8, 3, 3072], P(None, None, ('narrow', 'sub')), may hold values from -4 to 4
- timestep_index: int32 [2], P('groups'), parts along dimension 0, may hold values from 0 to 7
- cotangent: bfloat16 [1024, 3072], P(('groups', 'loop'), ('narrow', 'sub')), parts along dimension 0, may hold values from -0.25 to 0.25
Outputs:
- block_update: bfloat16 [1024, 3072], P(('groups', 'loop'), ('narrow', 'sub')), parts along dimension 0
- down_first_gradient: float32 [24576, 64], P(('groups', 'loop')), parts along dimension 0
- down_second_gradient: float32 [128, 3072], P('groups', ('narrow', 'sub')), parts along dimension 0
The draws below stay inside these ranges and needn't reach their ends.
There are 2 independent parts, one for each index of `groups`. The reference program is written for one: setup_inputs(seed, part) draws one part's arguments, and reference() takes and returns one part's arrays. A program takes and returns all parts, laid end to end along the dimension named above; an argument that names none is the same for every part. Nothing has to cross between parts.
All inputs are finite; a program needn't handle non-finite values.
Results may differ from the reference program's by a relative error of at most 0.02.
Values may be sent and summed in bfloat16 or wider, within the bound.
No kernel may reach another device: no remote copies, remote signals or barrier semaphores. Data moves between devices by JAX's collectives and lax.ppermute only.
A program may use at most 64 MiB of HBM per device.

```python
import math
import jax
import jax.numpy as jnp
from jax import lax

MODEL_WIDTH = 3072
HIDDEN_UNITS = 12288
ADAPTER_RANK = 64
STEPS = 8
SAMPLES = 1
ROWS = 512
N_LOOP = 4
N_NARROW = 2
N_SUB = 2


def draw_block_input_rows(key, part):
    key = jax.random.fold_in(key, 11)
    key_base, key_rows, key_cols = jax.random.split(key, 3)
    base_draw = jax.random.truncated_normal(key_base, -4.0, 4.0, (ROWS, MODEL_WIDTH), jnp.float32)
    row_scale = jnp.exp(jax.random.uniform(key_rows, (ROWS, 1), jnp.float32, 0.0, math.log(10.0)))
    col_scale = jnp.exp(jax.random.uniform(key_cols, (1, MODEL_WIDTH), jnp.float32, -0.6, 0.6))
    rising = jnp.exp(jnp.arange(MODEL_WIDTH, dtype=jnp.float32) * (math.log(3.0) / MODEL_WIDTH))[None, :]
    return (base_draw * row_scale * col_scale * rising).astype(jnp.bfloat16)


def block_levels(own_key, dims, pieces, low, top_value):
    level, own = 1.0, jax.random.fold_in(own_key, 6)
    for position, parts in pieces:
        heights = jnp.exp(jax.random.uniform(jax.random.fold_in(own, position), (parts,), jnp.float32, low / len(pieces), top_value / len(pieces)))
        level = level * jnp.repeat(heights, dims[position] // parts).reshape([-1 if axis == position else 1 for axis in range(len(dims))])
    return level


def scatter_about(rng, extent, spread, most, shards=(), kind=jnp.bfloat16):
    loudness = block_levels(rng, extent, shards, -0.22, 0.18) if shards else 1.0
    values = jax.random.normal(rng, extent, jnp.float32) * spread * loudness
    return jnp.minimum(jnp.maximum(values, -most), most).astype(kind)


def setup_inputs(seed: int = 0, part: int = 0) -> dict:
    arg_keys = jax.random.split(jax.random.key(seed), 9)
    own_keys = jax.random.split(jax.random.fold_in(arg_keys[8], part), 9)
    block_input_rows = draw_block_input_rows(jax.random.fold_in(jax.random.fold_in(arg_keys[8], part), 71), part)
    frozen_up_weight = scatter_about(arg_keys[1], (MODEL_WIDTH, HIDDEN_UNITS), MODEL_WIDTH ** -0.5, 0.109375, ((0, 4), (1, 4)))
    frozen_down_weight = scatter_about(arg_keys[2], (HIDDEN_UNITS, MODEL_WIDTH), HIDDEN_UNITS ** -0.5, 0.0546875, ((0, 4), (1, 4)))
    down_first_factor = scatter_about(arg_keys[3], (HIDDEN_UNITS, ADAPTER_RANK), HIDDEN_UNITS ** -0.5, 0.0546875)
    down_second_factor = scatter_about(arg_keys[4], (ADAPTER_RANK, MODEL_WIDTH), ADAPTER_RANK ** -0.5, 0.75)
    modulation = scatter_about(arg_keys[5], (STEPS, 3, MODEL_WIDTH), 0.7, 4.0, ((2, 4),), jnp.float32)
    timestep_index = jax.random.randint(own_keys[6], (SAMPLES,), 0, STEPS).astype(jnp.int32)
    cotangent = scatter_about(own_keys[7], (ROWS, MODEL_WIDTH), ROWS ** -0.5, 0.25, ((0, 4), (1, 4)))
    return dict(block_input_rows=block_input_rows, frozen_up_weight=frozen_up_weight, frozen_down_weight=frozen_down_weight, down_first_factor=down_first_factor, down_second_factor=down_second_factor, modulation=modulation, timestep_index=timestep_index, cotangent=cotangent)


adapter_scale = 0.5
norm_eps = 1e-06
gelu_coef = 0.7978845608028654

def gelu_value(pre_value):
    inner_arg = gelu_coef * (pre_value + 0.044715 * pre_value * pre_value * pre_value)
    return 0.5 * pre_value * (1.0 + jnp.tanh(inner_arg))

def block_partial_totals(left_block, right_block, block_count, out_cols):
    block_width = left_block.shape[1] // block_count

    def add_block(running, block_idx):
        left_part = lax.dynamic_slice_in_dim(left_block, block_idx * block_width, block_width, 1)
        right_part = lax.dynamic_slice_in_dim(right_block, block_idx * block_width, block_width, 0)
        partial_value = jnp.dot(left_part, right_part, preferred_element_type=jnp.float32).astype(jnp.bfloat16)
        partial_value = lax.optimization_barrier(partial_value)
        return (running + partial_value.astype(jnp.float32), None)
    running, _ = lax.scan(add_block, jnp.zeros((left_block.shape[0], out_cols), jnp.float32), jnp.arange(block_count, dtype=jnp.int32))
    return running

def reference(block_input_rows, frozen_up_weight, frozen_down_weight, down_first_factor, down_second_factor, modulation, timestep_index, cotangent):
    sample_of = jnp.arange(ROWS, dtype=jnp.int32) // (ROWS // SAMPLES)
    mod_rows = modulation[timestep_index[sample_of]]
    mod_shift = mod_rows[:, 0]
    mod_scale = mod_rows[:, 1]
    mod_gate = mod_rows[:, 2]
    input_f = block_input_rows.astype(jnp.float32)
    row_mean = lax.optimization_barrier(jnp.sum(input_f, axis=1)) / MODEL_WIDTH
    row_msq = lax.optimization_barrier(jnp.sum(input_f * input_f, axis=1)) / MODEL_WIDTH
    inv_std = lax.rsqrt(row_msq - row_mean * row_mean + norm_eps)
    normed = ((input_f - row_mean[:, None]) * inv_std[:, None] * (1.0 + mod_scale) + mod_shift).astype(jnp.bfloat16)
    pre_act = block_partial_totals(normed, frozen_up_weight, N_NARROW * N_SUB, HIDDEN_UNITS)
    activated_units = gelu_value(pre_act).astype(jnp.bfloat16)
    lowrank_down_output = block_partial_totals(activated_units, down_first_factor, N_LOOP, ADAPTER_RANK)
    frozen_down_output = block_partial_totals(activated_units, frozen_down_weight, N_LOOP, MODEL_WIDTH)
    branch_output = frozen_down_output + adapter_scale * jnp.dot(lowrank_down_output, down_second_factor.astype(jnp.float32), precision=lax.Precision.HIGHEST)
    block_update = (mod_gate * branch_output).astype(jnp.bfloat16)
    backward_rows = (mod_gate * cotangent.astype(jnp.float32)).astype(jnp.bfloat16)
    lowrank_backward = block_partial_totals(backward_rows, down_second_factor.T, N_NARROW * N_SUB, ADAPTER_RANK).astype(jnp.bfloat16)
    down_first_gradient = adapter_scale * jnp.dot(activated_units.T, lowrank_backward, preferred_element_type=jnp.float32)
    down_second_gradient = adapter_scale * jnp.dot(lowrank_down_output.T, backward_rows.astype(jnp.float32), precision=lax.Precision.HIGHEST)
    return (block_update, down_first_gradient, down_second_gradient)
```

```python
import jax
import jax.numpy as jnp
from jax import lax
from jax.sharding import PartitionSpec as P

adapter_scale = 0.5
norm_eps = 1e-06
gelu_coef = 0.7978845608028654
f32 = jnp.float32
bf16 = jnp.bfloat16


def gelu_value(pre_value):
    inner_arg = gelu_coef * (pre_value + 0.044715 * pre_value * pre_value * pre_value)
    return 0.5 * pre_value * (1.0 + jnp.tanh(inner_arg))


def dot(left, right):
    return jnp.dot(left, right, preferred_element_type=f32)


def swap(value, axis, distance):
    size = lax.axis_size(axis)
    return lax.ppermute(value, axis, [(i, i ^ distance) for i in range(size)])


def shift(value, axis, distance):
    size = lax.axis_size(axis)
    return lax.ppermute(value, axis, [(i, (i + distance) % size) for i in range(size)])


def sum_over(value, axis, kind):
    distance = 1
    while distance < lax.axis_size(axis):
        value = value.astype(kind)
        value = value.astype(f32) + swap(value, axis, distance).astype(f32)
        distance *= 2
    return value


def per_device(
    block_input_rows,
    frozen_up_weight,
    frozen_down_weight,
    down_first_factor,
    down_second_factor,
    modulation,
    timestep_index,
    cotangent,
):
    loop_size = lax.axis_size("loop")
    loop_position = lax.axis_index("loop")
    wide_position = lax.axis_index(("narrow", "sub"))
    sub_position = lax.axis_index("sub")
    wide_size = lax.axis_size("narrow") * lax.axis_size("sub")
    rows, features = block_input_rows.shape
    model_width = features * wide_size
    hidden = frozen_up_weight.shape[1]
    half = hidden // 2
    rank = down_first_factor.shape[1]
    first_factor = lax.dynamic_slice_in_dim(down_first_factor, loop_position * hidden, hidden, 0)
    second_factor = lax.dynamic_slice_in_dim(
        down_second_factor, wide_position * features, features, 1
    )
    step = lax.dynamic_index_in_dim(modulation, timestep_index[0], 0, keepdims=False)
    mod_shift, mod_scale, mod_gate = step[0:1], step[1:2], step[2:3]

    input_f = block_input_rows.astype(f32)
    back_rows = (mod_gate * cotangent.astype(f32)).astype(bf16)
    low_back_part = lax.dot_general(
        back_rows, second_factor, (((1,), (1,)), ((), ())), preferred_element_type=f32
    )
    packed = jnp.concatenate(
        [
            low_back_part,
            jnp.sum(input_f, axis=1, keepdims=True),
            jnp.sum(input_f * input_f, axis=1, keepdims=True),
        ],
        axis=1,
    )
    packed = sum_over(sum_over(packed, "sub", f32), "narrow", f32)
    row_mean = packed[:, rank : rank + 1] / model_width
    row_msq = packed[:, rank + 1 : rank + 2] / model_width
    low_back = packed[:, :rank].astype(bf16)
    inv_std = lax.rsqrt(row_msq - row_mean * row_mean + norm_eps)
    normed = ((input_f - row_mean) * inv_std * (1.0 + mod_scale) + mod_shift).astype(bf16)

    travelling = jnp.concatenate([normed, low_back], axis=1)
    first_gradient = None
    down_sum = None
    own_down = None
    for block in range(loop_size):
        block_normed = travelling[:, :features]
        block_low_back = travelling[:, features:]
        if block < loop_size - 1:
            travelling = shift(travelling, "loop", -1)
        up_part = dot(block_normed, frozen_up_weight).astype(bf16)
        kept = lax.dynamic_slice_in_dim(up_part, sub_position * half, half, 1)
        sent = lax.dynamic_slice_in_dim(up_part, (1 - sub_position) * half, half, 1)
        chip_sum = (kept.astype(f32) + swap(sent, "sub", 1).astype(f32)).astype(bf16)
        pre_act = sum_over(chip_sum, "narrow", bf16)
        own_half = gelu_value(pre_act).astype(bf16)
        other_half = swap(own_half, "sub", 1)
        activated = jnp.where(
            sub_position == 0,
            jnp.concatenate([own_half, other_half], axis=1),
            jnp.concatenate([other_half, own_half], axis=1),
        )
        low_part = dot(activated, first_factor)
        down_part = dot(activated, frozen_down_weight)
        joined = jnp.concatenate([down_part, low_part], axis=1)
        gradient_part = lax.dot_general(
            block_low_back, activated, (((0,), (0,)), ((), ())), preferred_element_type=f32
        )
        first_gradient = gradient_part if block == 0 else first_gradient + gradient_part
        if block == 0:
            own_down = joined.astype(bf16)
        else:
            if block > 1:
                joined = joined + down_sum.astype(f32)
            down_sum = shift(joined.astype(bf16), "loop", -1)
    total = own_down.astype(f32) + down_sum.astype(f32)
    base_down, low_down = total[:, :features], total[:, features:]
    branch = base_down + adapter_scale * jnp.dot(
        low_down, second_factor.astype(f32), precision=lax.Precision.HIGHEST
    )
    block_update = (mod_gate * branch).astype(bf16)
    contribution = adapter_scale * lax.dot_general(
        low_down,
        back_rows.astype(f32),
        (((0,), (0,)), ((), ())),
        preferred_element_type=f32,
        precision=lax.Precision.HIGHEST,
    )
    second_gradient = contribution.astype(bf16)
    if loop_size == 4:
        first, second, third = [shift(second_gradient, "loop", k).astype(f32) for k in (1, 2, 3)]
        second_gradient = (second_gradient.astype(f32) + second) + (first + third)
    else:
        second_gradient = lax.psum(second_gradient, "loop").astype(f32)
    return (block_update, adapter_scale * first_gradient.T, second_gradient)


def solution(mesh):
    in_specs = (
        P(("groups", "loop"), ("narrow", "sub")),
        P(("narrow", "sub"), "loop"),
        P("loop", ("narrow", "sub")),
        P(),
        P(),
        P(None, None, ("narrow", "sub")),
        P("groups"),
        P(("groups", "loop"), ("narrow", "sub")),
    )
    out_specs = (
        P(("groups", "loop"), ("narrow", "sub")),
        P(("groups", "loop"), None),
        P("groups", ("narrow", "sub")),
    )
    return jax.shard_map(
        per_device, mesh=mesh, in_specs=in_specs, out_specs=out_specs, check_vma=False
    )
```

```python
import functools

import jax
import jax.numpy as jnp
from jax import lax
from jax.experimental import pallas as pl
from jax.experimental.pallas import tpu as pltpu
from jax.sharding import PartitionSpec as P

adapter_scale = 0.5
norm_eps = 1e-06
gelu_coef = 0.7978845608028654
f32 = jnp.float32
bf16 = jnp.bfloat16
LANES = 128


def gelu_value(pre_value):
    inner_arg = gelu_coef * (pre_value + 0.044715 * pre_value * pre_value * pre_value)
    return 0.5 * pre_value * (1.0 + jnp.tanh(inner_arg))


def dot(left, right):
    return jnp.dot(left, right, preferred_element_type=f32)


def dot_transposed(left, right):
    return lax.dot_general(left, right, (((1,), (1,)), ((), ())), preferred_element_type=f32)


def dot_rows(left, right):
    return lax.dot_general(left, right, (((0,), (0,)), ((), ())), preferred_element_type=f32)


def split_dot(product, left, right):
    high = left.astype(bf16)
    low = (left - high.astype(f32)).astype(bf16)
    return product(high, right) + product(low, right)


def swap(value, axis, distance):
    size = lax.axis_size(axis)
    return lax.ppermute(value, axis, [(i, i ^ distance) for i in range(size)])


def shift(value, axis, distance):
    size = lax.axis_size(axis)
    return lax.ppermute(value, axis, [(i, (i + distance) % size) for i in range(size)])


def exchange(value, axis, kind):
    distance, size = 1, lax.axis_size(axis)
    while True:
        other = swap(value, axis, distance)
        distance *= 2
        if distance >= size:
            return value, other
        value = (value.astype(f32) + other.astype(f32)).astype(kind)


def call(body, outs, arrays, after=(), scratch=(), remote=(), scalars=(), grant=24 * 2**20):
    vmem = pl.BlockSpec(memory_space=pltpu.VMEM)
    specs = [pl.BlockSpec(memory_space=pltpu.SMEM)] * len(scalars)
    specs += [pl.BlockSpec(memory_space=pltpu.HBM)] * len(remote) + [vmem] * len(arrays)
    count = len(specs)
    specs += [pl.BlockSpec(memory_space=pl.ANY)] * len(after)
    total = len(specs)

    def kernel(*refs):
        body(*refs[:count], *refs[total:])

    return pl.pallas_call(
        kernel,
        out_shape=[jax.ShapeDtypeStruct(shape, kind) for shape, kind in outs],
        in_specs=specs,
        out_specs=[vmem] * len(outs),
        scratch_shapes=list(scratch),
        compiler_params=pltpu.CompilerParams(vmem_limit_bytes=grant),
        cost_estimate=pl.CostEstimate(flops=1024, bytes_accessed=1024, transcendentals=0),
        name=body.__name__,
    )(*scalars, *remote, *arrays, *after)


def cut(width):
    return width // 2 // LANES * LANES


def columns(width, step=512):
    return [slice(at, min(at + step, width)) for at in range(0, width, step)]


def rows_at(place, count):
    return pl.ds(pl.multiple_of(place * count, count), count)


def own_core():
    return lax.axis_index("sub")


def row_sums(step, x_hbm, cot_hbm, mod_hbm, second_hbm, packed, x, back, mod, factor, cot, table, sems):
    rows, features = x.shape
    rank = factor.shape[0]
    block = lax.axis_index("narrow") * lax.axis_size("sub") + lax.axis_index("sub")
    at = pl.ds(pl.multiple_of(block * features, LANES), features)
    copies = [
        pltpu.make_async_copy(mod_hbm, table, sems.at[0]),
        pltpu.make_async_copy(cot_hbm, cot, sems.at[1]),
        pltpu.make_async_copy(second_hbm.at[:, at], factor, sems.at[2]),
        pltpu.make_async_copy(x_hbm, x, sems.at[3]),
    ]
    for copy in copies:
        copy.start()
    copies[0].wait()
    for kind in range(3):
        mod[kind : kind + 1, :] = table[kind, pl.ds(step[0], 1), :]
    for copy in copies[1:]:
        copy.wait()
    back_rows = (mod[2:3, :] * cot[...].astype(f32)).astype(bf16)
    back[...] = back_rows
    padded = jnp.concatenate([factor[...], jnp.zeros((LANES - rank, features), bf16)], axis=0)
    low = dot_transposed(back_rows, padded)
    values = x[...].astype(f32)
    total = jnp.sum(values, axis=1, keepdims=True)
    squares = jnp.sum(values * values, axis=1, keepdims=True)
    lane = lax.broadcasted_iota(jnp.int32, (rows, LANES), 1)
    packed[...] = jnp.where(lane == rank, total, jnp.where(lane == rank + 1, squares, low))


def load_weight(weight_hbm, weight, sem):
    copy = pltpu.make_async_copy(weight_hbm, weight, sem)
    copy.start()
    copy.wait()


def add_packed(left, right, out):
    out[...] = left[...] + right[...]


def store_product(at, product, count, kept, left, right):
    kept[:, at] = product[:count]
    if at.start < left.shape[1]:
        left[:, at] = product[count:]
    else:
        right[:, slice(at.start - left.shape[1], at.stop - left.shape[1])] = product[count:]


def up_columns(width):
    middle = cut(width)
    return columns(middle) + [slice(at.start + middle, at.stop + middle) for at in columns(width - middle)]


def up_rows(normed, weight, kept, left, right):
    middle = normed.shape[0] // 2
    features = weight.shape[0]
    own = own_core()
    rows = jnp.concatenate(
        [normed[rows_at(own, middle), :features], normed[rows_at(1 - own, middle), :features]],
        axis=0,
    )
    for at in up_columns(weight.shape[1]):
        store_product(at, dot(rows, weight[:, at]).astype(bf16), middle, kept, left, right)


def normalize_up(model_width, rank, x, mine, other, mod, weight, travelling, kept, left, right):
    features = x.shape[1]
    packed = mine[...] + other[...]
    row_mean = packed[:, rank : rank + 1] / model_width
    row_msq = packed[:, rank + 1 : rank + 2] / model_width
    inv_std = lax.rsqrt(row_msq - row_mean * row_mean + norm_eps)
    travelling[:, :features] = (
        (x[...].astype(f32) - row_mean) * inv_std * (1.0 + mod[1:2, :]) + mod[0:1, :]
    ).astype(bf16)
    travelling[:, features:] = packed.astype(bf16)
    quarter = x.shape[0] // 4
    own = own_core()
    rows = jnp.concatenate(
        [
            travelling[rows_at(own, quarter), :features],
            travelling[rows_at(2 + own, quarter), :features],
            travelling[rows_at(1 - own, quarter), :features],
            travelling[rows_at(3 - own, quarter), :features],
        ],
        axis=0,
    )
    for at in up_columns(weight.shape[1]):
        product = dot(rows, weight[:, at]).astype(bf16)
        store_product(at, product, 2 * quarter, kept, left, right)


def sum_rows(kept, left, right, rows, out):
    middle = left.shape[1]
    out[:, :middle] = (kept[rows, :middle].astype(f32) + left[rows, :].astype(f32)).astype(bf16)
    out[:, middle:] = (kept[rows, middle:].astype(f32) + right[rows, :].astype(f32)).astype(bf16)


def add_own(kept, left, right, travelling, first, last, passed):
    middle = first.shape[0]
    sum_rows(kept, left, right, slice(0, middle), first)
    sum_rows(kept, left, right, slice(middle, 2 * middle), last)
    passed[...] = travelling[...]


def add_cores(kept, left, right, out):
    sum_rows(kept, left, right, slice(0, out.shape[0]), out)


def add_cores_pass(kept, left, right, last, out, passed):
    sum_rows(kept, left, right, slice(0, out.shape[0]), out)
    passed[...] = last[...]


def gelu_rows(mine, other, left, right):
    width = left.shape[1]
    for out, base in ((left, 0), (right, width)):
        for at in columns(out.shape[1]):
            source = slice(at.start + base, at.stop + base)
            pre_act = mine[:, source].astype(f32) + other[:, source].astype(f32)
            out[:, at] = gelu_value(pre_act).astype(bf16)


def two_halves(own, other):
    return [jnp.concatenate([a[...], b[...]], axis=0) for a, b in zip(own, other)]


def low_product(activated, first):
    left, right = activated
    hidden = left.shape[1] + right.shape[1]
    base = lax.axis_index("loop") * hidden
    factor_left = first[:, pl.ds(pl.multiple_of(base, LANES), left.shape[1])]
    factor_right = first[:, pl.ds(pl.multiple_of(base + left.shape[1], LANES), right.shape[1])]
    return dot_transposed(left, factor_left) + dot_transposed(right, factor_right)


def down_product(activated, weight, at):
    left, right = activated
    middle = left.shape[1]
    return dot(left, weight[:middle, at]) + dot(right, weight[middle:, at])


def store_rows(out, at, value):
    middle = value.shape[0] // 2
    own = own_core()
    out[rows_at(own, middle), at] = value[:middle].astype(out.dtype)
    out[rows_at(1 - own, middle), at] = value[middle:].astype(out.dtype)


def down_rows(left, right, other_left, other_right, weight, first, out):
    activated = two_halves((left, right), (other_left, other_right))
    features = weight.shape[1]
    low = low_product(activated, first)
    low = jnp.concatenate([low, jnp.zeros((low.shape[0], LANES - low.shape[1]), f32)], axis=1)
    store_rows(out, slice(features, features + LANES), low)
    for at in columns(features, 256):
        store_rows(out, at, down_product(activated, weight, at))


def down_rows_add(left, right, other_left, other_right, weight, first, received, out, total):
    down_rows(left, right, other_left, other_right, weight, first, total)
    out[...] = (total[...] + received[...].astype(f32)).astype(bf16)


def down_own(left, right, other_left, other_right, weight, first, out):
    middle = out.shape[0] // 2
    down_rows(left, right, other_left, other_right, weight, first, out.at[:middle])
    out[middle:] = jnp.zeros((middle, out.shape[1]), f32)


def down_own_add(left, right, other_left, other_right, weight, first, received, out):
    down_own(left, right, other_left, other_right, weight, first, out)
    out[...] += received[...].astype(f32)


def first_gradient_part(*refs):
    blocks, out = refs[:-1], refs[-1]
    own = own_core()
    rank = out.shape[0]
    features = blocks[4].shape[1] - LANES
    middle = blocks[0].shape[1]
    factors = []
    for at in range(0, len(blocks), 5):
        count = blocks[at].shape[0]
        travelling = blocks[at + 4]
        factors += [travelling[rows_at(own, count), features:], travelling[rows_at(1 - own, count), features:]]
    factors = jnp.concatenate(factors, axis=0)
    for half, base in ((0, 0), (1, middle)):
        for at in columns(blocks[half].shape[1]):
            right = []
            for place in range(0, len(blocks), 5):
                right += [blocks[place + half][:, at], blocks[place + 2 + half][:, at]]
            product = dot_rows(factors, jnp.concatenate(right, axis=0))
            out[:, slice(at.start + base, at.stop + base)] = product[:rank]


def first_gradient_end(left, right, other_left, other_right, travelling, part, out):
    own = own_core()
    rank = out.shape[0]
    count = left.shape[0]
    features = travelling.shape[1] - LANES
    factors = jnp.concatenate(
        [travelling[rows_at(2 + own, count), features:], travelling[rows_at(3 - own, count), features:]],
        axis=0,
    )
    base = 0
    for mine, other in ((left, other_left), (right, other_right)):
        for at in columns(mine.shape[1]):
            product = dot_rows(factors, jnp.concatenate([mine[:, at], other[:, at]], axis=0))
            to = slice(at.start + base, at.stop + base)
            out[:, to] = adapter_scale * (part[:, to] + product[:rank])
        base += mine.shape[1]


def second_gradient_part(
    left, right, other_left, other_right, first, own_down, received, back, out, low_total, low
):
    activated = two_halves((left, right), (other_left, other_right))
    rank = first.shape[0]
    features = back.shape[1]
    store_rows(low, slice(0, rank), low_product(activated, first))
    sums = received[:, features : features + rank].astype(f32) + own_down[:, features : features + rank]
    middle = low.shape[0]
    sums = jnp.concatenate([sums[:middle], sums[middle:] + low[...]], axis=0)
    low_total[...] = sums
    out[...] = (adapter_scale * split_dot(dot_rows, sums, back[...])).astype(bf16)


def update_rows(
    left, right, other_left, other_right, weight, own_down, received, low_total, factor, mod, out, total
):
    activated = two_halves((left, right), (other_left, other_right))
    features = weight.shape[1]
    for at in columns(features, 256):
        store_rows(total, at, down_product(activated, weight, at))
    gate = mod[2:3, :]
    low = adapter_scale * split_dot(dot, low_total[...], factor[...])
    base = received[:, :features].astype(f32) + own_down[:, :features] + low
    middle = total.shape[0]
    out[:middle] = (gate * base[:middle]).astype(bf16)
    out[middle:] = (gate * (base[middle:] + total[...])).astype(bf16)


def add_four(own, one, two, three, out):
    out[...] = (own[...].astype(f32) + two[...].astype(f32)) + (
        one[...].astype(f32) + three[...].astype(f32)
    )


def per_device(
    block_input_rows,
    frozen_up_weight,
    frozen_down_weight,
    down_first_factor,
    down_second_factor,
    modulation,
    timestep_index,
    cotangent,
):
    loop_size = lax.axis_size("loop")
    wide_size = lax.axis_size("narrow") * lax.axis_size("sub")
    rows, features = block_input_rows.shape
    hidden = frozen_up_weight.shape[1]
    rank = down_first_factor.shape[1]
    middle, quarter = rows // 2, rows // 4
    wide = features + LANES
    first = down_first_factor.T
    part = cut(hidden)
    dma = pltpu.SemaphoreType.DMA

    def swap_halves(left, right):
        return [swap(left, "sub", 1), swap(right, "sub", 1)]

    packed, x, back, mod, second = call(
        row_sums,
        [
            ((rows, LANES), f32),
            ((rows, features), bf16),
            ((rows, features), bf16),
            ((8, features), f32),
            ((rank, features), bf16),
        ],
        [],
        scratch=[
            pltpu.VMEM((rows, features), bf16),
            pltpu.VMEM((3, modulation.shape[0], features), f32),
            dma((4,)),
        ],
        scalars=[timestep_index],
        remote=[block_input_rows, cotangent, jnp.transpose(modulation, (1, 0, 2)), down_second_factor],
    )
    (packed,) = call(
        add_packed, [((rows, LANES), f32)], [packed, swap(packed, "sub", 1)], [back]
    )
    (up_weight,) = call(
        load_weight,
        [((features, hidden), bf16)],
        [],
        [packed],
        scratch=[dma],
        remote=[frozen_up_weight],
    )
    mine, other = exchange(packed, "narrow", f32)
    body = functools.partial(normalize_up, wide_size * features, rank)
    body.__name__ = "normalize_up"

    def halves(count):
        return [((count, part), bf16), ((count, hidden - part), bf16)]

    travelling, kept, left, right = call(
        body,
        [((rows, wide), bf16), ((middle, hidden), bf16), *halves(middle)],
        [x, mine, other, mod, up_weight],
    )
    first_sum, last_sum, travelling = call(
        add_own,
        [((quarter, hidden), bf16), ((quarter, hidden), bf16), ((rows, wide), bf16)],
        [kept, *swap_halves(left, right), travelling],
    )
    first_pair = exchange(first_sum, "narrow", bf16)
    if loop_size == 4:
        near, far = swap(travelling, "loop", 1), swap(travelling, "loop", 2)
        blocks = [near, swap(far, "loop", 1), far]
    else:
        blocks = [travelling]
        for _ in range(loop_size - 1):
            blocks.append(shift(blocks[-1], "loop", -1))
        blocks = blocks[1:]
    pairs = []
    activated = []

    def activate(pair, after):
        left, right = call(gelu_rows, halves(pair[0].shape[0]), list(pair), after)
        activated.append([left, right, *swap_halves(left, right)])
        return activated[-1]

    after = [first_sum]
    for place, block in enumerate(blocks):
        if place == 2:
            after = activate(pairs[0], after)[:1]
        kept, left, right = call(
            up_rows,
            [((middle, hidden), bf16), *halves(middle)],
            [block, up_weight],
            after,
        )
        after = [kept]
        if place == 0:
            after = activate(first_pair, after)
        operands = [kept, *swap_halves(left, right)]
        if place < loop_size - 2:
            (value,) = call(add_cores, [((middle, hidden), bf16)], operands, after)
        else:
            value, last_sum = call(
                add_cores_pass,
                [((middle, hidden), bf16), ((quarter, hidden), bf16)],
                [*operands, last_sum],
                after,
            )
        after = [value]
        pairs.append(exchange(value, "narrow", bf16))
    last_pair = exchange(last_sum, "narrow", bf16)

    down_sum = None
    own_down = None
    for place in range(loop_size - 1):
        if len(activated) < place + 2:
            after = activate(pairs[place], after)[:1]
        operands = [*activated[place + 1], frozen_down_weight, first]
        if down_sum is None:
            (joined,) = call(down_rows, [((rows, wide), bf16)], operands, after)
        else:
            (joined,) = call(
                down_rows_add,
                [((rows, wide), bf16)],
                [*operands, down_sum],
                after,
                scratch=[pltpu.VMEM((rows, wide), f32)],
            )
        after = [joined]
        operands = [*activated[0], frozen_down_weight, first]
        if loop_size != 4:
            down_sum = shift(joined, "loop", -1)
            if place == 0:
                (own_down,) = call(down_own, [((rows, wide), f32)], operands, after)
                after = [own_down]
        elif place == 0:
            own_part = swap(joined, "loop", 1)
        elif place == 1:
            down_sum = swap(joined, "loop", 1)
            (own_down,) = call(down_own_add, [((rows, wide), f32)], [*operands, own_part], after)
            after = [own_down]
        else:
            down_sum = swap(joined, "loop", 2)
    gathered = []
    for parts, block in zip(activated, [travelling] + blocks):
        gathered += [*parts, block]
    (gradient,) = call(first_gradient_part, [((rank, hidden), f32)], gathered, after)
    last = activate(last_pair, [gradient])
    contribution, low_total = call(
        second_gradient_part,
        [((rank, features), bf16), ((rows, rank), f32)],
        [*last, first, own_down, down_sum, back],
        scratch=[pltpu.VMEM((middle, rank), f32)],
    )
    (block_update,) = call(
        update_rows,
        [((rows, features), bf16)],
        [*last, frozen_down_weight, own_down, down_sum, low_total, second, mod],
        scratch=[pltpu.VMEM((middle, features), f32)],
    )
    (first_gradient,) = call(
        first_gradient_end,
        [((rank, hidden), f32)],
        [*last, travelling, gradient],
        [low_total],
    )
    if loop_size == 4:
        others = [shift(contribution, "loop", k) for k in (1, 2, 3)]
        (second_gradient,) = call(
            add_four, [((rank, features), f32)], [contribution, *others], [block_update]
        )
    else:
        second_gradient = lax.psum(contribution, "loop").astype(f32)
    return (block_update, first_gradient.T, second_gradient)


def solution(mesh):
    in_specs = (
        P(("groups", "loop"), ("narrow", "sub")),
        P(("narrow", "sub"), "loop"),
        P("loop", ("narrow", "sub")),
        P(),
        P(),
        P(None, None, ("narrow", "sub")),
        P("groups"),
        P(("groups", "loop"), ("narrow", "sub")),
    )
    out_specs = (
        P(("groups", "loop"), ("narrow", "sub")),
        P(("groups", "loop"), None),
        P("groups", ("narrow", "sub")),
    )
    return jax.shard_map(
        per_device, mesh=mesh, in_specs=in_specs, out_specs=out_specs, check_vma=False
    )
```

```python
import functools

import jax
import jax.numpy as jnp
from jax import lax
from jax.experimental import pallas as pl
from jax.experimental.pallas import tpu as pltpu
from jax.sharding import PartitionSpec as P

adapter_scale = 0.5
norm_eps = 1e-06
gelu_coef = 0.7978845608028654
f32 = jnp.float32
bf16 = jnp.bfloat16
LANES = 128
ORDER = [2, 3, 1]
OWN_GRANT = (64 * 1024 - 11400) * 1024


def gelu_value(pre_value):
    inner_arg = gelu_coef * (pre_value + 0.044715 * pre_value * pre_value * pre_value)
    return 0.5 * pre_value * (1.0 + jnp.tanh(inner_arg))


def dot(left, right):
    return jnp.dot(left, right, preferred_element_type=f32)


def dot_transposed(left, right):
    return lax.dot_general(left, right, (((1,), (1,)), ((), ())), preferred_element_type=f32)


def dot_rows(left, right):
    return lax.dot_general(left, right, (((0,), (0,)), ((), ())), preferred_element_type=f32)


def split_dot(product, left, right):
    high = left.astype(bf16)
    low = (left - high.astype(f32)).astype(bf16)
    return product(high, right) + product(low, right)


def swap(value, axis, distance):
    size = lax.axis_size(axis)
    return lax.ppermute(value, axis, [(i, i ^ distance) for i in range(size)])


def exchange(value, axis, kind):
    distance, size = 1, lax.axis_size(axis)
    while True:
        other = swap(value, axis, distance)
        distance *= 2
        if distance >= size:
            return value, other
        value = (value.astype(f32) + other.astype(f32)).astype(kind)


def call(body, outs, arrays, after=(), scratch=(), remote=(), scalars=(), grant=24 * 2**20):
    vmem = pl.BlockSpec(memory_space=pltpu.VMEM)
    specs = [pl.BlockSpec(memory_space=pltpu.SMEM)] * len(scalars)
    specs += [pl.BlockSpec(memory_space=pltpu.HBM)] * len(remote) + [vmem] * len(arrays)
    count = len(specs)
    specs += [pl.BlockSpec(memory_space=pl.ANY)] * len(after)
    total = len(specs)

    def kernel(*refs):
        body(*refs[:count], *refs[total:])

    return pl.pallas_call(
        kernel,
        out_shape=[jax.ShapeDtypeStruct(shape, kind) for shape, kind in outs],
        in_specs=specs,
        out_specs=[vmem] * len(outs),
        scratch_shapes=list(scratch),
        compiler_params=pltpu.CompilerParams(vmem_limit_bytes=grant),
        cost_estimate=pl.CostEstimate(flops=1024, bytes_accessed=1024, transcendentals=0),
        name=body.__name__,
    )(*scalars, *remote, *arrays, *after)


def cut(width):
    return width // 2 // LANES * LANES


def columns(width, step=512):
    return [slice(at, min(at + step, width)) for at in range(0, width, step)]


def rows_at(place, count):
    return pl.ds(pl.multiple_of(place * count, count), count)


def own_core():
    return lax.axis_index("sub")


def feature_block():
    return lax.axis_index("narrow") * lax.axis_size("sub") + lax.axis_index("sub")


def centred(x, mod):
    values = x[...].astype(f32)
    total = jnp.sum(values, axis=1, keepdims=True)
    rows = (values - total / x.shape[1]) * (1.0 + mod[1:2, :])
    return rows.astype(bf16), total, values


def split_rows(value):
    high = value.astype(bf16)
    return [high, (value - high.astype(f32)).astype(bf16)]


def order_rows(value):
    middle = value.shape[0] // 2
    low, high = value[:middle], value[middle:]
    own = own_core()
    return [jnp.where(own == 0, low, high), jnp.where(own == 0, high, low)]


def own_rows(
    step, x_hbm, cot_hbm, mod_hbm, second_hbm, weight_hbm,
    kept_left, kept_right, left, right, packed, factor, mod, weight, x, cot, table, sems,
):
    rows, features = x.shape
    rank = factor.shape[0]
    hidden = weight.shape[1]
    tiles = hidden // LANES
    block = feature_block()
    blocks = lax.axis_size("narrow") * lax.axis_size("sub")
    at = pl.ds(pl.multiple_of(block * features, LANES), features)
    copies = [
        pltpu.make_async_copy(mod_hbm, table, sems.at[0]),
        pltpu.make_async_copy(x_hbm, x, sems.at[1]),
        pltpu.make_async_copy(cot_hbm, cot, sems.at[2]),
        pltpu.make_async_copy(second_hbm.at[:, at], factor, sems.at[3]),
    ]
    pieces = up_columns(hidden)
    loads = [
        pltpu.make_async_copy(weight_hbm.at[:, piece], weight.at[:, piece], sems.at[4 + place])
        for place, piece in enumerate(pieces)
    ]
    for copy in copies + loads:
        copy.start()
    copies[0].wait()
    for kind in range(3):
        mod[kind : kind + 1, :] = table[kind, pl.ds(step[0], 1), :]
    copies[1].wait()
    normed, total, values = centred(x, mod)
    squares = jnp.sum(values * values, axis=1, keepdims=True)
    extra = split_rows(1.0 + mod[1:2, :]) + split_rows(mod[0:1, :])
    extra.append(jnp.zeros((16 - len(extra), features), bf16))
    left_rows = jnp.concatenate(order_rows(normed) + extra, axis=0)
    for copy in copies[2:]:
        copy.wait()
    back_rows = (mod[2:3, :] * cot[...].astype(f32)).astype(bf16)
    padded = jnp.concatenate([factor[...], jnp.zeros((LANES - rank, features), bf16)], axis=0)
    low = dot_transposed(back_rows, padded)
    lane = lax.broadcasted_iota(jnp.int32, (rows, LANES), 1)
    low = jnp.where(lane == rank + block, total, low)
    packed[:rows] = jnp.where(lane == rank + blocks, squares, low)
    packed[rows:] = jnp.zeros((packed.shape[0] - rows, LANES), f32)
    middle = rows // 2
    for piece, load in zip(pieces, loads):
        load.wait()
        product = dot(left_rows, weight[:, piece])
        store_product(piece, product[:rows].astype(bf16), middle, kept_left, kept_right, left, right)
        scale_row = product[rows : rows + 1] + product[rows + 1 : rows + 2]
        shift_row = product[rows + 2 : rows + 3] + product[rows + 3 : rows + 4]
        for tile in range((piece.stop - piece.start) // LANES):
            lanes = slice(tile * LANES, (tile + 1) * LANES)
            place = piece.start // LANES + tile
            packed[pl.ds(rows + block * tiles + place, 1), :] = scale_row[:, lanes]
            packed[rows + blocks * tiles + place : rows + blocks * tiles + place + 1, :] = shift_row[:, lanes]


def add_packed(left, right, out):
    out[...] = left[...] + right[...]


def unpack(left, right, stats, table):
    rows, tiles = stats.shape[0], table.shape[1] // LANES
    stats[...] = left[:rows] + right[:rows]
    count = (left.shape[0] - rows) // tiles
    for kind in range(count):
        for tile in range(tiles):
            at = slice(rows + kind * tiles + tile, rows + kind * tiles + tile + 1)
            table[kind : kind + 1, tile * LANES : (tile + 1) * LANES] = left[at] + right[at]


def store_product(at, product, count, kept_left, kept_right, left, right):
    if at.start < left.shape[1]:
        kept_left[:, at] = product[:count]
        left[:, at] = product[count:]
    else:
        to = slice(at.start - left.shape[1], at.stop - left.shape[1])
        kept_right[:, to] = product[:count]
        right[:, to] = product[count:]


def up_columns(width):
    middle = cut(width)
    return columns(middle) + [slice(at.start + middle, at.stop + middle) for at in columns(width - middle)]


def up_rows(x, mod, weight, kept_left, kept_right, left, right):
    count = x.shape[0]
    normed, _, _ = centred(x, mod)
    rows = jnp.concatenate(order_rows(normed), axis=0)
    for at in up_columns(weight.shape[1]):
        product = dot(rows, weight[:, at]).astype(bf16)
        store_product(at, product, count // 2, kept_left, kept_right, left, right)


def add_cores(kept_left, kept_right, left, right, out):
    middle = left.shape[1]
    out[:, :middle] = (kept_left[...].astype(f32) + left[...].astype(f32)).astype(bf16)
    out[:, middle:] = (kept_right[...].astype(f32) + right[...].astype(f32)).astype(bf16)


def gelu_rows(rank, features, mine, other, stats, table, left, right):
    width, count = left.shape[1], left.shape[0]
    blocks = lax.axis_size("narrow") * lax.axis_size("sub")
    rows = stats[pl.ds(pl.multiple_of(own_core() * count, 16), count), :]
    sums = [rows[:, rank + block : rank + block + 1] for block in range(blocks)]
    row_mean = sum(sums[1:], sums[0]) / (blocks * features)
    row_msq = rows[:, rank + blocks : rank + blocks + 1] / (blocks * features)
    inv_std = lax.rsqrt(row_msq - row_mean * row_mean + norm_eps)
    offsets = [value / features - row_mean for value in sums]
    for out, start in ((left, 0), (right, width)):
        for at in columns(out.shape[1]):
            source = slice(at.start + start, at.stop + start)
            value = mine[:, source].astype(f32) + other[:, source].astype(f32)
            for block in range(blocks):
                value = value + offsets[block] * table[block : block + 1, source]
            pre_act = inv_std * value + table[blocks : blocks + 1, source]
            out[:, at] = gelu_value(pre_act).astype(bf16)


def two_halves(own, other):
    return [jnp.concatenate([a[...], b[...]], axis=0) for a, b in zip(own, other)]


def low_product(activated, first):
    left, right = activated
    hidden = left.shape[1] + right.shape[1]
    base = lax.axis_index("loop") * hidden
    factor_left = first[:, pl.ds(pl.multiple_of(base, LANES), left.shape[1])]
    factor_right = first[:, pl.ds(pl.multiple_of(base + left.shape[1], LANES), right.shape[1])]
    return dot_transposed(left, factor_left) + dot_transposed(right, factor_right)


def down_product(activated, weight, at):
    left, right = activated
    middle = left.shape[1]
    return dot(left, weight[:middle, at]) + dot(right, weight[middle:, at])


def store_rows(out, at, value):
    middle = value.shape[0] // 2
    own = own_core()
    out[rows_at(own, middle), at] = value[:middle].astype(out.dtype)
    out[rows_at(1 - own, middle), at] = value[middle:].astype(out.dtype)


def down_rows(left, right, other_left, other_right, weight, first, out):
    activated = two_halves((left, right), (other_left, other_right))
    features = weight.shape[1]
    low = low_product(activated, first)
    low = jnp.concatenate([low, jnp.zeros((low.shape[0], LANES - low.shape[1]), f32)], axis=1)
    store_rows(out, slice(features, features + LANES), low)
    for at in columns(features, 256):
        store_rows(out, at, down_product(activated, weight, at))


def stat_rows(stats, count):
    own = own_core()
    return [
        stats[pl.ds(pl.multiple_of(place * count, 16), count), :].astype(bf16)
        for place in (own, 1 - own)
    ]


def first_gradient_rows(*refs):
    blocks, out = refs[:-1], refs[-1]
    rank = out.shape[0]
    middle = blocks[0].shape[1]
    factors = []
    for at in range(0, len(blocks), 5):
        factors += stat_rows(blocks[at + 4], blocks[at].shape[0])
    factors = jnp.concatenate(factors, axis=0)
    for half, base in ((0, 0), (1, middle)):
        for at in columns(blocks[half].shape[1]):
            right = []
            for place in range(0, len(blocks), 5):
                right += [blocks[place + half][:, at], blocks[place + 2 + half][:, at]]
            product = dot_rows(factors, jnp.concatenate(right, axis=0))
            out[:, slice(at.start + base, at.stop + base)] = adapter_scale * product[:rank]


def second_gradient_part(left, right, other_left, other_right, first, cot, mod, *refs):
    received, (out, low_total, low) = refs[:-3], refs[-3:]
    activated = two_halves((left, right), (other_left, other_right))
    rank = first.shape[0]
    features = cot.shape[1]
    lanes = slice(features, features + rank)
    back_rows = (mod[2:3, :] * cot[...].astype(f32)).astype(bf16)
    store_rows(low, slice(0, rank), low_product(activated, first))
    sums = low[...]
    for value in received:
        sums = sums + value[:, lanes].astype(f32)
    low_total[...] = sums
    out[...] = (adapter_scale * split_dot(dot_rows, sums, back_rows)).astype(bf16)


def update_rows(left, right, other_left, other_right, weight, low_total, factor, mod, *refs):
    received, (out, total) = refs[:-2], refs[-2:]
    activated = two_halves((left, right), (other_left, other_right))
    features = factor.shape[1]
    for at in columns(features, 256):
        store_rows(total, at, down_product(activated, weight, at))
    base = total[...] + adapter_scale * split_dot(dot, low_total[...], factor[...])
    for value in received:
        base = base + value[:, :features].astype(f32)
    out[...] = (mod[2:3, :] * base).astype(bf16)


def add_four(own, one, two, three, out):
    out[...] = (own[...].astype(f32) + one[...].astype(f32)) + (
        two[...].astype(f32) + three[...].astype(f32)
    )


def per_device(
    block_input_rows,
    frozen_up_weight,
    frozen_down_weight,
    down_first_factor,
    down_second_factor,
    modulation,
    timestep_index,
    cotangent,
):
    loop_size = lax.axis_size("loop")
    wide_size = lax.axis_size("narrow") * lax.axis_size("sub")
    rows, features = block_input_rows.shape
    hidden = frozen_up_weight.shape[1]
    rank = down_first_factor.shape[1]
    blocks = wide_size
    middle = rows // 2
    wide = features + LANES
    first = down_first_factor.T
    part = cut(hidden)
    tiles = hidden // LANES
    dma = pltpu.SemaphoreType.DMA

    def swap_halves(left, right):
        return [swap(left, "sub", 1), swap(right, "sub", 1)]

    def halves(count):
        return [((count, part), bf16), ((count, hidden - part), bf16)]

    def named(body, *values):
        bound = functools.partial(body, *values)
        bound.__name__ = body.__name__
        return bound

    order = ORDER if loop_size == 4 else list(range(1, loop_size))
    raw = {k: swap(block_input_rows, "loop", k) for k in range(1, min(loop_size, 3))}
    for k in range(3, loop_size):
        raw[k] = swap(raw[2] if k == 3 else block_input_rows, "loop", 1 if k == 3 else k)

    length = -(-(rows + (blocks + 1) * tiles) // 8) * 8
    *kept, left, right, packed, second, mod = call(
        own_rows,
        [
            *halves(middle),
            *halves(middle),
            ((length, LANES), f32),
            ((rank, features), bf16),
            ((8, features), f32),
        ],
        [],
        scratch=[
            pltpu.VMEM((features, hidden), bf16),
            pltpu.VMEM((rows, features), bf16),
            pltpu.VMEM((rows, features), bf16),
            pltpu.VMEM((3, modulation.shape[0], features), f32),
            dma((4 + len(up_columns(hidden)),)),
        ],
        scalars=[timestep_index],
        remote=[
            block_input_rows,
            cotangent,
            jnp.transpose(modulation, (1, 0, 2)),
            down_second_factor,
            frozen_up_weight,
        ],
        grant=OWN_GRANT,
    )
    (packed,) = call(add_packed, [((length, LANES), f32)], [packed, swap(packed, "sub", 1)])
    own_stats, table = call(
        unpack,
        [((rows, LANES), f32), ((-(-(blocks + 1) // 8) * 8, hidden), f32)],
        list(exchange(packed, "narrow", f32)),
    )
    stats = [swap(own_stats, "loop", k) for k in order] + [own_stats]
    pairs = []
    activated = []
    received = []

    def multiply(place, after):
        *kept, left, right = call(
            up_rows,
            [*halves(middle), *halves(middle)],
            [raw[order[place]], mod, frozen_up_weight],
            after,
        )
        return [*kept, *swap_halves(left, right)]

    def add(parts, after):
        (value,) = call(add_cores, [((middle, hidden), bf16)], parts, after)
        pairs.append(exchange(value, "narrow", bf16))
        return [value]

    def activate(after):
        place = len(activated)
        left, right = call(
            named(gelu_rows, rank, features),
            halves(middle),
            [*pairs[place], stats[place], table],
            after,
        )
        activated.append([left, right, *swap_halves(left, right)])
        return [left]

    def down(place, after):
        operands = [*activated[place], frozen_down_weight, first]
        (joined,) = call(down_rows, [((rows, wide), bf16)], operands, after + received[-1:])
        received.append(swap(joined, "loop", order[place]))
        return [joined]

    own_parts = [*kept, *swap_halves(left, right)]
    last = len(order)
    after = [packed]
    for place in range(last):
        if place >= 2:
            after = activate(after) + stats[1:-1]
        parts = multiply(place, after)
        after = parts[:1]
        if place == 0:
            after = after + [own_stats]
        if place >= 2:
            after = down(place - 2, after)
        after = add(parts, after)
    after = add(own_parts, after)
    for place in (last - 2, last - 1):
        after = activate(after)
        after = down(place, after)
    after = activate(after)
    own = activated[last]
    contribution, low_total = call(
        second_gradient_part,
        [((rank, features), bf16), ((rows, rank), f32)],
        [*own, first, cotangent, mod, *received],
        after,
        scratch=[pltpu.VMEM((rows, rank), f32)],
    )
    (block_update,) = call(
        update_rows,
        [((rows, features), bf16)],
        [*own, frozen_down_weight, low_total, second, mod, *received],
        scratch=[pltpu.VMEM((rows, features), f32)],
    )
    gathered = []
    for parts, rows_of in zip(activated, stats):
        gathered += [*parts, rows_of]
    (first_gradient,) = call(first_gradient_rows, [((rank, hidden), f32)], gathered, [low_total])
    if loop_size == 4:
        terms = [swap(contribution, "loop", k) for k in (1, 2, 3)]
        (second_gradient,) = call(
            add_four, [((rank, features), f32)], [contribution, *terms], [block_update]
        )
    else:
        second_gradient = lax.psum(contribution, "loop").astype(f32)
    return (block_update, first_gradient.T, second_gradient)


def solution(mesh):
    in_specs = (
        P(("groups", "loop"), ("narrow", "sub")),
        P(("narrow", "sub"), "loop"),
        P("loop", ("narrow", "sub")),
        P(),
        P(),
        P(None, None, ("narrow", "sub")),
        P("groups"),
        P(("groups", "loop"), ("narrow", "sub")),
    )
    out_specs = (
        P(("groups", "loop"), ("narrow", "sub")),
        P(("groups", "loop"), None),
        P("groups", ("narrow", "sub")),
    )
    return jax.shard_map(
        per_device, mesh=mesh, in_specs=in_specs, out_specs=out_specs, check_vma=False
    )
```

```python
import functools

import jax
import jax.numpy as jnp
from jax import lax
from jax.experimental import pallas as pl
from jax.experimental.pallas import tpu as pltpu
from jax.sharding import PartitionSpec as P

adapter_scale = 0.5
norm_eps = 1e-06
gelu_coef = 0.7978845608028654
f32 = jnp.float32
bf16 = jnp.bfloat16
LANES = 128
TOUCHES = 2
ORDER = [2, 3, 1]
OWN_PIECES = 3
UP_PIECES = (4, 2, 2)
OWN_PLACE = 0
GELU_PIECES = 2
OWN_GRANT = (64 * 1024 - 11440) * 1024


def gelu_value(pre_value):
    inner_arg = gelu_coef * (pre_value + 0.044715 * pre_value * pre_value * pre_value)
    return 0.5 * pre_value * (1.0 + jnp.tanh(inner_arg))


def dot(left, right):
    return jnp.dot(left, right, preferred_element_type=f32)


def dot_transposed(left, right):
    return lax.dot_general(left, right, (((1,), (1,)), ((), ())), preferred_element_type=f32)


def dot_rows(left, right):
    return lax.dot_general(left, right, (((0,), (0,)), ((), ())), preferred_element_type=f32)


def split_dot(product, left, right):
    high = left.astype(bf16)
    low = (left - high.astype(f32)).astype(bf16)
    return product(high, right) + product(low, right)


def swap(value, axis, distance):
    size = lax.axis_size(axis)
    return lax.ppermute(value, axis, [(i, i ^ distance) for i in range(size)])


def exchange(value, axis, kind):
    distance, size = 1, lax.axis_size(axis)
    while True:
        other = swap(value, axis, distance)
        distance *= 2
        if distance >= size:
            return value, other
        value = (value.astype(f32) + other.astype(f32)).astype(kind)


def call(body, outs, arrays, after=(), scratch=(), remote=(), scalars=(), grant=24 * 2**20):
    vmem = pl.BlockSpec(memory_space=pltpu.VMEM)
    specs = [pl.BlockSpec(memory_space=pltpu.SMEM)] * len(scalars)
    specs += [pl.BlockSpec(memory_space=pltpu.HBM)] * len(remote) + [vmem] * len(arrays)
    count = len(specs)
    specs += [pl.BlockSpec(memory_space=pl.ANY)] * len(after)
    total = len(specs)

    def kernel(*refs):
        body(*refs[:count], *refs[total:])

    results = pl.pallas_call(
        kernel,
        out_shape=[jax.ShapeDtypeStruct(shape, kind) for shape, kind in outs],
        in_specs=specs,
        out_specs=[vmem] * len(outs),
        scratch_shapes=list(scratch),
        compiler_params=pltpu.CompilerParams(vmem_limit_bytes=grant),
        cost_estimate=pl.CostEstimate(flops=1024, bytes_accessed=1024, transcendentals=0),
        name=body.__name__,
    )(*scalars, *remote, *arrays, *after)
    return list(results)


def pieces(width, count):
    tiles = width // LANES
    count = min(count, tiles)
    return [(tiles * (k + 1) // count - tiles * k // count) * LANES for k in range(count)]


def bases(arrays):
    at = 0
    for array in arrays:
        yield array, at
        at += array.shape[1]


def unit_pieces(arrays):
    for place, (array, base) in enumerate(bases(arrays)):
        yield array, base, array.shape[1] - (LANES if place == len(arrays) - 1 else 0)


def columns(width, step=512):
    return [slice(at, min(at + step, width)) for at in range(0, width, step)]


def rows_at(place, count):
    return pl.ds(pl.multiple_of(place * count, count), count)


def own_core():
    return lax.axis_index("sub")


def feature_block():
    return lax.axis_index("narrow") * lax.axis_size("sub") + lax.axis_index("sub")


def centred(x, mod):
    values = x[...].astype(f32)
    total = jnp.sum(values, axis=1, keepdims=True)
    rows = (values - total / x.shape[1]) * (1.0 + mod[1:2, :])
    return rows.astype(bf16), total, values


def three_terms(value):
    high = value.astype(bf16).astype(f32)
    middle = (value - high).astype(bf16).astype(f32)
    return [high, middle, value - high - middle]


def sum_lanes(values, total):
    squares = jnp.sum(values * values, axis=1, keepdims=True)
    lane = lax.broadcasted_iota(jnp.int32, (values.shape[0], LANES), 1) - 8 * feature_block()
    lanes = jnp.zeros((values.shape[0], LANES), f32)
    for place, term in enumerate(three_terms(total) + three_terms(squares)):
        lanes = jnp.where(lane == place, term, lanes)
    return lanes.astype(bf16)


def split_rows(value):
    high = value.astype(bf16)
    return [high, (value - high.astype(f32)).astype(bf16)]


def order_rows(value):
    middle = value.shape[0] // 2
    low, high = value[:middle], value[middle:]
    own = own_core()
    return [jnp.where(own == 0, low, high), jnp.where(own == 0, high, low)]


def own_rows(step, x_hbm, cot_hbm, mod_hbm, second_hbm, weight_hbm, *refs):
    *parts, packed, factor, mod, weight, x, cot, table, sems = refs
    kept, sent = parts[: len(parts) // 2], parts[len(parts) // 2 :]
    rows, features = x.shape
    rank = factor.shape[0]
    hidden = weight.shape[1]
    tiles = hidden // LANES
    block = feature_block()
    blocks = lax.axis_size("narrow") * lax.axis_size("sub")
    at = pl.ds(pl.multiple_of(block * features, LANES), features)
    copies = [
        pltpu.make_async_copy(mod_hbm, table, sems.at[0]),
        pltpu.make_async_copy(x_hbm, x, sems.at[1]),
        pltpu.make_async_copy(cot_hbm, cot, sems.at[2]),
        pltpu.make_async_copy(second_hbm.at[:, at], factor, sems.at[3]),
    ]
    loads = []
    for _, base, width in unit_pieces(kept):
        at = slice(base, base + width)
        loads.append(pltpu.make_async_copy(weight_hbm.at[:, at], weight.at[:, at], sems.at[4 + len(loads)]))
    for copy in copies + loads:
        copy.start()
    copies[0].wait()
    for kind in range(3):
        mod[kind : kind + 1, :] = table[kind, pl.ds(step[0], 1), :]
    copies[1].wait()
    normed, total, values = centred(x, mod)
    lanes = jnp.concatenate(order_rows(sum_lanes(values, total)), axis=0)
    extra = split_rows(1.0 + mod[1:2, :]) + split_rows(mod[0:1, :])
    extra.append(jnp.zeros((16 - len(extra), features), bf16))
    left_rows = jnp.concatenate(order_rows(normed) + extra, axis=0)
    for copy in copies[2:]:
        copy.wait()
    back_rows = (mod[2:3, :] * cot[...].astype(f32)).astype(bf16)
    padded = jnp.concatenate([jnp.zeros((LANES - rank, features), bf16), factor[...]], axis=0)
    packed[:rows] = dot_transposed(back_rows, padded)
    packed[rows:] = jnp.zeros((packed.shape[0] - rows, LANES), f32)
    middle = rows // 2
    kept[-1][:, -LANES:] = lanes[:middle]
    sent[-1][:, -LANES:] = lanes[middle:]
    for (piece, base, width), other, load in zip(unit_pieces(kept), sent, loads):
        load.wait()
        for at in columns(width):
            product = dot(left_rows, weight[:, base + at.start : base + at.stop])
            piece[:, at] = product[:middle].astype(bf16)
            other[:, at] = product[middle:rows].astype(bf16)
            scale_row = product[rows : rows + 1] + product[rows + 1 : rows + 2]
            shift_row = product[rows + 2 : rows + 3] + product[rows + 3 : rows + 4]
            for tile in range((at.stop - at.start) // LANES):
                lanes = slice(tile * LANES, (tile + 1) * LANES)
                place = rows + (base + at.start) // LANES + tile
                packed[pl.ds(place + block * tiles, 1), :] = scale_row[:, lanes]
                packed[place + blocks * tiles : place + blocks * tiles + 1, :] = shift_row[:, lanes]


def add_packed(left, right, out):
    out[...] = left[...] + right[...]


def unpack(left, right, low_back, table):
    rows, tiles = low_back.shape[0], table.shape[1] // LANES
    low_back[...] = (left[:rows] + right[:rows]).astype(bf16)
    count = (left.shape[0] - rows) // tiles
    for kind in range(count):
        for tile in range(tiles):
            at = slice(rows + kind * tiles + tile, rows + kind * tiles + tile + 1)
            table[kind : kind + 1, tile * LANES : (tile + 1) * LANES] = left[at] + right[at]


def up_rows(x, mod, weight, *parts):
    kept, sent = parts[: len(parts) // 2], parts[len(parts) // 2 :]
    middle = x.shape[0] // 2
    normed, total, values = centred(x, mod)
    rows = jnp.concatenate(order_rows(normed), axis=0)
    lanes = jnp.concatenate(order_rows(sum_lanes(values, total)), axis=0)
    kept[-1][:, -LANES:] = lanes[:middle]
    sent[-1][:, -LANES:] = lanes[middle:]
    for (piece, base, width), other in zip(unit_pieces(kept), sent):
        for at in columns(width):
            product = dot(rows, weight[:, base + at.start : base + at.stop]).astype(bf16)
            piece[:, at] = product[:middle]
            other[:, at] = product[middle:]


def add_cores(*refs):
    *parts, out = refs
    kept, received = parts[: len(parts) // 2], parts[len(parts) // 2 :]
    for (piece, base), other in zip(bases(kept), received):
        total = piece[...].astype(f32) + other[...].astype(f32)
        out[:, base : base + piece.shape[1]] = total.astype(bf16)


def touch(out):
    out[...] = jnp.zeros_like(out)


def gelu_rows(features, mine, other, table, *parts):
    blocks = lax.axis_size("narrow") * lax.axis_size("sub")
    lanes = mine[:, -LANES:].astype(f32) + other[:, -LANES:].astype(f32)

    def term(place):
        return lanes[:, place : place + 1] + lanes[:, place + 1 : place + 2] + lanes[:, place + 2 : place + 3]

    sums = [term(8 * block) for block in range(blocks)]
    squares = [term(8 * block + 3) for block in range(blocks)]
    row_mean = sum(sums[1:], sums[0]) / (blocks * features)
    row_msq = sum(squares[1:], squares[0]) / (blocks * features)
    inv_std = lax.rsqrt(row_msq - row_mean * row_mean + norm_eps)
    offsets = [value / features - row_mean for value in sums]
    for out, start in bases(parts):
        for at in columns(out.shape[1]):
            source = slice(at.start + start, at.stop + start)
            value = mine[:, source].astype(f32) + other[:, source].astype(f32)
            for block in range(blocks):
                value = value + offsets[block] * table[block : block + 1, source]
            pre_act = inv_std * value + table[blocks : blocks + 1, source]
            out[:, at] = gelu_value(pre_act).astype(bf16)


def both_cores(parts):
    count = len(parts) // 2
    return [jnp.concatenate([a[...], b[...]], axis=0) for a, b in zip(parts[:count], parts[count:])]


def low_product(activated, first):
    hidden = sum(piece.shape[1] for piece in activated)
    place = lax.axis_index("loop") * hidden
    terms = []
    for piece, base in bases(activated):
        at = pl.ds(pl.multiple_of(place + base, LANES), piece.shape[1])
        terms.append(dot_transposed(piece, first[:, at]))
    return sum(terms[1:], terms[0])


def down_product(activated, weight, at):
    terms = [dot(piece, weight[base : base + piece.shape[1], at]) for piece, base in bases(activated)]
    return sum(terms[1:], terms[0])


def store_rows(out, at, value):
    middle = value.shape[0] // 2
    own = own_core()
    out[rows_at(own, middle), at] = value[:middle].astype(out.dtype)
    out[rows_at(1 - own, middle), at] = value[middle:].astype(out.dtype)


def down_rows(weight, first, low_back, *refs):
    *parts, out = refs
    activated = both_cores(parts)
    features = weight.shape[1]
    low = low_product(activated, first)
    low = jnp.concatenate([low, jnp.zeros((low.shape[0], LANES - low.shape[1]), f32)], axis=1)
    last = slice(features, features + LANES)
    store_rows(out, last, low)
    out[:, last] = (out[:, last].astype(f32) + low_back[...].astype(f32)).astype(bf16)
    for at in columns(features, 256):
        store_rows(out, at, down_product(activated, weight, at))


def first_gradient_rows(count, *refs):
    *blocks, out = refs
    rank = out.shape[0]
    stride = 2 * count + 1
    places = range(0, len(blocks), stride)
    own = own_core()
    factors = []
    for at in places:
        middle = blocks[at].shape[0]
        low_back = blocks[at + stride - 1]
        factors += [low_back[rows_at(core, middle), -LANES:] for core in (own, 1 - own)]
    factors = jnp.concatenate(factors, axis=0)
    for which, (piece, base) in enumerate(bases(blocks[:count])):
        for at in columns(piece.shape[1]):
            right = []
            for place in places:
                right += [blocks[place + which][:, at], blocks[place + count + which][:, at]]
            product = dot_rows(factors, jnp.concatenate(right, axis=0))
            out[:, slice(at.start + base, at.stop + base)] = adapter_scale * product[LANES - rank :]


def second_gradient_part(terms, first, cot, mod, *refs):
    *arrays, out, low_total, low = refs
    received, parts = arrays[:terms], arrays[terms:]
    rank, features = first.shape[0], cot.shape[1]
    back_rows = (mod[2:3, :] * cot[...].astype(f32)).astype(bf16)
    store_rows(low, slice(0, rank), low_product(both_cores(parts), first))
    sums = low[...]
    for value in received:
        sums = sums + value[:, features : features + rank].astype(f32)
    low_total[...] = sums
    out[...] = (adapter_scale * split_dot(dot_rows, sums, back_rows)).astype(bf16)


def update_rows(terms, weight, low_total, factor, mod, *refs):
    *arrays, out, total = refs
    received, parts = arrays[:terms], arrays[terms:]
    activated = both_cores(parts)
    features = factor.shape[1]
    for at in columns(features, 256):
        store_rows(total, at, down_product(activated, weight, at))
    base = total[...] + adapter_scale * split_dot(dot, low_total[...], factor[...])
    for value in received:
        base = base + value[:, :features].astype(f32)
    out[...] = (mod[2:3, :] * base).astype(bf16)


def add_four(own, one, two, three, out):
    out[...] = (own[...].astype(f32) + one[...].astype(f32)) + (
        two[...].astype(f32) + three[...].astype(f32)
    )


def per_device(
    block_input_rows,
    frozen_up_weight,
    frozen_down_weight,
    down_first_factor,
    down_second_factor,
    modulation,
    timestep_index,
    cotangent,
):
    loop_size = lax.axis_size("loop")
    wide_size = lax.axis_size("narrow") * lax.axis_size("sub")
    rows, features = block_input_rows.shape
    hidden = frozen_up_weight.shape[1]
    rank = down_first_factor.shape[1]
    blocks = wide_size
    middle = rows // 2
    wide = features + LANES
    first = down_first_factor.T
    tiles = hidden // LANES
    dma = pltpu.SemaphoreType.DMA

    def swap_all(parts):
        return [swap(part, "sub", 1) for part in parts]

    def cut(count, extra=0):
        widths = pieces(hidden, count)
        widths[-1] += extra
        return [((middle, width), bf16) for width in widths]

    def named(body, *values):
        bound = functools.partial(body, *values)
        bound.__name__ = body.__name__
        return bound

    order = ORDER if loop_size == 4 else list(range(1, loop_size))
    raw = {k: swap(block_input_rows, "loop", k) for k in range(1, min(loop_size, 3))}
    for k in range(3, loop_size):
        raw[k] = swap(raw[2] if k == 3 else block_input_rows, "loop", 1 if k == 3 else k)

    length = -(-(rows + (blocks + 1) * tiles) // 8) * 8
    *own_parts, packed, second, mod = call(
        own_rows,
        [
            *(2 * cut(OWN_PIECES, LANES)),
            ((length, LANES), f32),
            ((rank, features), bf16),
            ((8, features), f32),
        ],
        [],
        scratch=[
            pltpu.VMEM((features, hidden), bf16),
            pltpu.VMEM((rows, features), bf16),
            pltpu.VMEM((rows, features), bf16),
            pltpu.VMEM((3, modulation.shape[0], features), f32),
            dma((4 + OWN_PIECES,)),
        ],
        scalars=[timestep_index],
        remote=[
            block_input_rows,
            cotangent,
            jnp.transpose(modulation, (1, 0, 2)),
            down_second_factor,
            frozen_up_weight,
        ],
        grant=OWN_GRANT,
    )
    (packed,) = call(add_packed, [((length, LANES), f32)], [packed, swap(packed, "sub", 1)])
    low_back, table = call(
        unpack,
        [((rows, LANES), bf16), ((-(-(blocks + 1) // 8) * 8, hidden), f32)],
        list(exchange(packed, "narrow", f32)),
    )
    pairs = []
    activated = []
    received = []

    def cores(parts):
        count = len(parts) // 2
        return parts[:count] + swap_all(parts[count:])

    def multiply(place, after):
        return call(
            up_rows, 2 * cut(UP_PIECES[min(place, 2)], LANES), [raw[order[place]], mod, frozen_up_weight], after
        )

    def add(parts, after):
        (value,) = call(add_cores, [((middle, hidden + LANES), bf16)], cores(parts), after)
        pairs.append(exchange(value, "narrow", bf16))
        return [value]

    def activate(after):
        place = len(activated)
        parts = call(
            named(gelu_rows, features),
            cut(GELU_PIECES),
            [*pairs[place], table],
            after,
        )
        activated.append([*parts, *swap_all(parts)])
        return parts[:1]

    def down(place, after):
        operands = [frozen_down_weight, first, low_back, *activated[place]]
        (joined,) = call(down_rows, [((rows, wide), bf16)], operands, after)
        received.append(swap(joined, "loop", order[place]))
        return [joined]

    def wait(after):
        return call(touch, [((8, LANES), f32)], [], after)

    last = len(order)
    after = [packed]
    for place in range(last):
        if place >= 2:
            after = activate(after)
        parts = multiply(place, after)
        after = parts[:1]
        if place == 0:
            after = after + [table]
        if place >= 2:
            after = down(place - 2, after)
        after = add(parts, after)
        if place == OWN_PLACE:
            after = add(own_parts, after)
            own_pair = pairs.pop()
    after = activate(after)
    after = wait(after + received[-1:])
    if OWN_PLACE > 2:
        after = add(own_parts, after)
        own_pair = pairs.pop()
    else:
        for _ in range(TOUCHES):
            after = wait(after)
    after = down(last - 2, after)
    after = activate(after)
    after = wait(down(last - 1, after) + received[-2:-1])
    pairs.append(own_pair)
    after = activate(after)
    own = activated[last]
    contribution, low_total = call(
        named(second_gradient_part, last),
        [((rank, features), bf16), ((rows, rank), f32)],
        [first, cotangent, mod, *received, *own],
        after,
        scratch=[pltpu.VMEM((rows, rank), f32)],
    )
    (block_update,) = call(
        named(update_rows, last),
        [((rows, features), bf16)],
        [frozen_down_weight, low_total, second, mod, *received, *own],
        scratch=[pltpu.VMEM((rows, features), f32)],
    )
    gathered = []
    for parts, rows_of in zip(activated, received + [low_back]):
        gathered += [*parts, rows_of]
    (first_gradient,) = call(
        named(first_gradient_rows, len(cut(GELU_PIECES))),
        [((rank, hidden), f32)],
        gathered,
        [low_total],
    )
    if loop_size == 4:
        terms = [swap(contribution, "loop", k) for k in (1, 2, 3)]
        (second_gradient,) = call(
            add_four,
            [((rank, features), f32)],
            [contribution, *terms],
            [low_total],
        )
    else:
        second_gradient = lax.psum(contribution, "loop").astype(f32)
    return (block_update, first_gradient.T, second_gradient)


def solution(mesh):
    in_specs = (
        P(("groups", "loop"), ("narrow", "sub")),
        P(("narrow", "sub"), "loop"),
        P("loop", ("narrow", "sub")),
        P(),
        P(),
        P(None, None, ("narrow", "sub")),
        P("groups"),
        P(("groups", "loop"), ("narrow", "sub")),
    )
    out_specs = (
        P(("groups", "loop"), ("narrow", "sub")),
        P(("groups", "loop"), None),
        P("groups", ("narrow", "sub")),
    )
    return jax.shard_map(
        per_device, mesh=mesh, in_specs=in_specs, out_specs=out_specs, check_vma=False
    )
```

```python
import functools

import jax
import jax.numpy as jnp
from jax import lax
from jax.experimental import pallas as pl
from jax.experimental.pallas import tpu as pltpu
from jax.sharding import PartitionSpec as P

adapter_scale = 0.5
norm_eps = 1e-06
gelu_coef = 0.7978845608028654
f32 = jnp.float32
bf16 = jnp.bfloat16
LANES = 128
TOUCHES = 2
ORDER = [2, 3, 1]
OWN_PIECES = 3
UP_PIECES = (4, 2, 2)
OWN_PLACE = 0
GELU_PIECES = 2
OWN_GRANT = (64 * 1024 - 11440) * 1024


def gelu_value(pre_value):
    inner_arg = gelu_coef * (pre_value + 0.044715 * pre_value * pre_value * pre_value)
    return 0.5 * pre_value * (1.0 + jnp.tanh(inner_arg))


def dot(left, right):
    return jnp.dot(left, right, preferred_element_type=f32)


def dot_transposed(left, right):
    return lax.dot_general(left, right, (((1,), (1,)), ((), ())), preferred_element_type=f32)


def dot_rows(left, right):
    return lax.dot_general(left, right, (((0,), (0,)), ((), ())), preferred_element_type=f32)


def split_dot(product, left, right):
    high = left.astype(bf16)
    low = (left - high.astype(f32)).astype(bf16)
    return product(high, right) + product(low, right)


def swap(value, axis, distance):
    size = lax.axis_size(axis)
    return lax.ppermute(value, axis, [(i, i ^ distance) for i in range(size)])


def exchange(value, axis, kind):
    distance, size = 1, lax.axis_size(axis)
    while True:
        other = swap(value, axis, distance)
        distance *= 2
        if distance >= size:
            return value, other
        value = (value.astype(f32) + other.astype(f32)).astype(kind)


def call(body, outs, arrays, after=(), scratch=(), remote=(), scalars=(), grant=24 * 2**20):
    vmem = pl.BlockSpec(memory_space=pltpu.VMEM)
    specs = [pl.BlockSpec(memory_space=pltpu.SMEM)] * len(scalars)
    specs += [pl.BlockSpec(memory_space=pltpu.HBM)] * len(remote) + [vmem] * len(arrays)
    count = len(specs)
    specs += [pl.BlockSpec(memory_space=pl.ANY)] * len(after)
    total = len(specs)

    def kernel(*refs):
        body(*refs[:count], *refs[total:])

    results = pl.pallas_call(
        kernel,
        out_shape=[jax.ShapeDtypeStruct(shape, kind) for shape, kind in outs],
        in_specs=specs,
        out_specs=[vmem] * len(outs),
        scratch_shapes=list(scratch),
        compiler_params=pltpu.CompilerParams(vmem_limit_bytes=grant),
        cost_estimate=pl.CostEstimate(flops=1024, bytes_accessed=1024, transcendentals=0),
        name=body.__name__,
    )(*scalars, *remote, *arrays, *after)
    return list(results)


def pieces(width, count):
    tiles = width // LANES
    count = min(count, tiles)
    return [(tiles * (k + 1) // count - tiles * k // count) * LANES for k in range(count)]


def bases(arrays):
    at = 0
    for array in arrays:
        yield array, at
        at += array.shape[1]


def unit_pieces(arrays):
    for place, (array, base) in enumerate(bases(arrays)):
        yield array, base, array.shape[1] - (LANES if place == len(arrays) - 1 else 0)


def columns(width, step=512):
    return [slice(at, min(at + step, width)) for at in range(0, width, step)]


def rows_at(place, count):
    return pl.ds(pl.multiple_of(place * count, count), count)


def own_core():
    return lax.axis_index("sub")


def feature_block():
    return lax.axis_index("narrow") * lax.axis_size("sub") + lax.axis_index("sub")


def centred(x, mod):
    values = x[...].astype(f32)
    total = jnp.sum(values, axis=1, keepdims=True)
    rows = (values - total / x.shape[1]) * (1.0 + mod[1:2, :])
    return rows.astype(bf16), total, values


def three_terms(value):
    high = value.astype(bf16).astype(f32)
    middle = (value - high).astype(bf16).astype(f32)
    return [high, middle, value - high - middle]


def sum_lanes(values, total):
    squares = jnp.sum(values * values, axis=1, keepdims=True)
    lane = lax.broadcasted_iota(jnp.int32, (values.shape[0], LANES), 1) - 8 * feature_block()
    lanes = jnp.zeros((values.shape[0], LANES), f32)
    for place, term in enumerate(three_terms(total) + three_terms(squares)):
        lanes = jnp.where(lane == place, term, lanes)
    return lanes.astype(bf16)


def split_rows(value):
    high = value.astype(bf16)
    return [high, (value - high.astype(f32)).astype(bf16)]


def order_rows(value):
    middle = value.shape[0] // 2
    low, high = value[:middle], value[middle:]
    own = own_core()
    return [jnp.where(own == 0, low, high), jnp.where(own == 0, high, low)]


def own_rows(step, x_hbm, cot_hbm, mod_hbm, second_hbm, weight_hbm, *refs):
    *parts, packed, factor, mod, weight, x, cot, table, sems = refs
    kept, sent = parts[: len(parts) // 2], parts[len(parts) // 2 :]
    rows, features = x.shape
    rank = factor.shape[0]
    hidden = weight.shape[1]
    tiles = hidden // LANES
    block = feature_block()
    blocks = lax.axis_size("narrow") * lax.axis_size("sub")
    at = pl.ds(pl.multiple_of(block * features, LANES), features)
    copies = [
        pltpu.make_async_copy(mod_hbm, table, sems.at[0]),
        pltpu.make_async_copy(x_hbm, x, sems.at[1]),
        pltpu.make_async_copy(cot_hbm, cot, sems.at[2]),
        pltpu.make_async_copy(second_hbm.at[:, at], factor, sems.at[3]),
    ]
    loads = []
    for _, base, width in unit_pieces(kept):
        at = slice(base, base + width)
        loads.append(pltpu.make_async_copy(weight_hbm.at[:, at], weight.at[:, at], sems.at[4 + len(loads)]))
    for copy in copies + loads:
        copy.start()
    copies[0].wait()
    for kind in range(3):
        mod[kind : kind + 1, :] = table[kind, pl.ds(step[0], 1), :]
    copies[1].wait()
    normed, total, values = centred(x, mod)
    lanes = jnp.concatenate(order_rows(sum_lanes(values, total)), axis=0)
    extra = split_rows(1.0 + mod[1:2, :]) + split_rows(mod[0:1, :])
    extra.append(jnp.zeros((16 - len(extra), features), bf16))
    left_rows = jnp.concatenate(order_rows(normed) + extra, axis=0)
    for copy in copies[2:]:
        copy.wait()
    back_rows = (mod[2:3, :] * cot[...].astype(f32)).astype(bf16)
    padded = jnp.concatenate([jnp.zeros((LANES - rank, features), bf16), factor[...]], axis=0)
    packed[:rows] = dot_transposed(back_rows, padded)
    packed[rows:] = jnp.zeros((packed.shape[0] - rows, LANES), f32)
    middle = rows // 2
    kept[-1][:, -LANES:] = lanes[:middle]
    sent[-1][:, -LANES:] = lanes[middle:]
    for (piece, base, width), other, load in zip(unit_pieces(kept), sent, loads):
        load.wait()
        for at in columns(width):
            product = dot(left_rows, weight[:, base + at.start : base + at.stop])
            piece[:, at] = product[:middle].astype(bf16)
            other[:, at] = product[middle:rows].astype(bf16)
            scale_row = product[rows : rows + 1] + product[rows + 1 : rows + 2]
            shift_row = product[rows + 2 : rows + 3] + product[rows + 3 : rows + 4]
            for tile in range((at.stop - at.start) // LANES):
                lanes = slice(tile * LANES, (tile + 1) * LANES)
                place = rows + (base + at.start) // LANES + tile
                packed[pl.ds(place + block * tiles, 1), :] = scale_row[:, lanes]
                packed[place + blocks * tiles : place + blocks * tiles + 1, :] = shift_row[:, lanes]


def add_packed(left, right, out):
    out[...] = left[...] + right[...]


def unpack(left, right, low_back, table):
    rows, tiles = low_back.shape[0], table.shape[1] // LANES
    low_back[...] = (left[:rows] + right[:rows]).astype(bf16)
    count = (left.shape[0] - rows) // tiles
    for kind in range(count):
        for tile in range(tiles):
            at = slice(rows + kind * tiles + tile, rows + kind * tiles + tile + 1)
            table[kind : kind + 1, tile * LANES : (tile + 1) * LANES] = left[at] + right[at]


def up_rows(x, mod, weight, *parts):
    kept, sent = parts[: len(parts) // 2], parts[len(parts) // 2 :]
    middle = x.shape[0] // 2
    normed, total, values = centred(x, mod)
    rows = jnp.concatenate(order_rows(normed), axis=0)
    lanes = jnp.concatenate(order_rows(sum_lanes(values, total)), axis=0)
    kept[-1][:, -LANES:] = lanes[:middle]
    sent[-1][:, -LANES:] = lanes[middle:]
    for (piece, base, width), other in zip(unit_pieces(kept), sent):
        for at in columns(width):
            product = dot(rows, weight[:, base + at.start : base + at.stop]).astype(bf16)
            piece[:, at] = product[:middle]
            other[:, at] = product[middle:]


def add_cores(*refs):
    *parts, out = refs
    kept, received = parts[: len(parts) // 2], parts[len(parts) // 2 :]
    for (piece, base), other in zip(bases(kept), received):
        total = piece[...].astype(f32) + other[...].astype(f32)
        out[:, base : base + piece.shape[1]] = total.astype(bf16)


def touch(out):
    out[...] = jnp.zeros_like(out)


def gelu_rows(features, mine, other, table, *parts):
    blocks = lax.axis_size("narrow") * lax.axis_size("sub")
    lanes = mine[:, -LANES:].astype(f32) + other[:, -LANES:].astype(f32)

    def term(place):
        return lanes[:, place : place + 1] + lanes[:, place + 1 : place + 2] + lanes[:, place + 2 : place + 3]

    sums = [term(8 * block) for block in range(blocks)]
    squares = [term(8 * block + 3) for block in range(blocks)]
    row_mean = sum(sums[1:], sums[0]) / (blocks * features)
    row_msq = sum(squares[1:], squares[0]) / (blocks * features)
    inv_std = lax.rsqrt(row_msq - row_mean * row_mean + norm_eps)
    offsets = [value / features - row_mean for value in sums]
    for out, start in bases(parts):
        for at in columns(out.shape[1]):
            source = slice(at.start + start, at.stop + start)
            value = mine[:, source].astype(f32) + other[:, source].astype(f32)
            for block in range(blocks):
                value = value + offsets[block] * table[block : block + 1, source]
            pre_act = inv_std * value + table[blocks : blocks + 1, source]
            out[:, at] = gelu_value(pre_act).astype(bf16)


def both_cores(parts):
    count = len(parts) // 2
    return [jnp.concatenate([a[...], b[...]], axis=0) for a, b in zip(parts[:count], parts[count:])]


def low_product(activated, first):
    hidden = sum(piece.shape[1] for piece in activated)
    place = lax.axis_index("loop") * hidden
    terms = []
    for piece, base in bases(activated):
        at = pl.ds(pl.multiple_of(place + base, LANES), piece.shape[1])
        terms.append(dot_transposed(piece, first[:, at]))
    return sum(terms[1:], terms[0])


def down_product(activated, weight, at):
    terms = [dot(piece, weight[base : base + piece.shape[1], at]) for piece, base in bases(activated)]
    return sum(terms[1:], terms[0])


def store_rows(out, at, value):
    middle = value.shape[0] // 2
    own = own_core()
    out[rows_at(own, middle), at] = value[:middle].astype(out.dtype)
    out[rows_at(1 - own, middle), at] = value[middle:].astype(out.dtype)


def down_rows(weight, first, low_back, *refs):
    *parts, out = refs
    activated = both_cores(parts)
    features = weight.shape[1]
    low = low_product(activated, first)
    low = jnp.concatenate([low, jnp.zeros((low.shape[0], LANES - low.shape[1]), f32)], axis=1)
    last = slice(features, features + LANES)
    store_rows(out, last, low)
    out[:, last] = (out[:, last].astype(f32) + low_back[...].astype(f32)).astype(bf16)
    for at in columns(features, 256):
        store_rows(out, at, down_product(activated, weight, at))


def first_gradient_rows(count, *refs):
    *blocks, out, done = refs
    done[...] = jnp.zeros_like(done)
    rank = out.shape[0]
    stride = 2 * count + 1
    places = range(0, len(blocks), stride)
    own = own_core()
    factors = []
    for at in places:
        middle = blocks[at].shape[0]
        low_back = blocks[at + stride - 1]
        factors += [low_back[rows_at(core, middle), -LANES:] for core in (own, 1 - own)]
    factors = jnp.concatenate(factors, axis=0)
    for which, (piece, base) in enumerate(bases(blocks[:count])):
        for at in columns(piece.shape[1]):
            right = []
            for place in places:
                right += [blocks[place + which][:, at], blocks[place + count + which][:, at]]
            product = dot_rows(factors, jnp.concatenate(right, axis=0))
            out[:, slice(at.start + base, at.stop + base)] = adapter_scale * product[LANES - rank :]


def second_gradient_part(terms, first, cot, mod, *refs):
    *arrays, upper, lower, low_total, low = refs
    received, parts = arrays[:terms], arrays[terms:]
    rank, features = first.shape[0], cot.shape[1]
    back_rows = (mod[2:3, :] * cot[...].astype(f32)).astype(bf16)
    store_rows(low, slice(0, rank), low_product(both_cores(parts), first))
    sums = low[...]
    for value in received:
        sums = sums + value[:, features : features + rank].astype(f32)
    low_total[...] = sums
    product = (adapter_scale * split_dot(dot_rows, sums, back_rows)).astype(bf16)
    upper[...] = product[: rank // 2]
    lower[...] = product[rank // 2 :]


def update_rows(terms, weight, low_total, factor, mod, *refs):
    *arrays, out, total = refs
    received, parts = arrays[:terms], arrays[terms:]
    activated = both_cores(parts)
    features = factor.shape[1]
    for at in columns(features, 256):
        store_rows(total, at, down_product(activated, weight, at))
    base = total[...] + adapter_scale * split_dot(dot, low_total[...], factor[...])
    for value in received:
        base = base + value[:, :features].astype(f32)
    out[...] = (mod[2:3, :] * base).astype(bf16)


def add_pair(left, right, out):
    out[...] = (left[...].astype(f32) + right[...].astype(f32)).astype(out.dtype)


def add_halves(upper, upper_other, lower, lower_other, out):
    middle = upper.shape[0]
    out[:middle] = upper[...].astype(f32) + upper_other[...].astype(f32)
    out[middle:] = lower[...].astype(f32) + lower_other[...].astype(f32)


def per_device(
    block_input_rows,
    frozen_up_weight,
    frozen_down_weight,
    down_first_factor,
    down_second_factor,
    modulation,
    timestep_index,
    cotangent,
):
    loop_size = lax.axis_size("loop")
    wide_size = lax.axis_size("narrow") * lax.axis_size("sub")
    rows, features = block_input_rows.shape
    hidden = frozen_up_weight.shape[1]
    rank = down_first_factor.shape[1]
    blocks = wide_size
    middle = rows // 2
    wide = features + LANES
    first = down_first_factor.T
    tiles = hidden // LANES
    dma = pltpu.SemaphoreType.DMA

    def swap_all(parts):
        return [swap(part, "sub", 1) for part in parts]

    def cut(count, extra=0):
        widths = pieces(hidden, count)
        widths[-1] += extra
        return [((middle, width), bf16) for width in widths]

    def named(body, *values):
        bound = functools.partial(body, *values)
        bound.__name__ = body.__name__
        return bound

    order = ORDER if loop_size == 4 else list(range(1, loop_size))
    raw = {k: swap(block_input_rows, "loop", k) for k in range(1, min(loop_size, 3))}
    for k in range(3, loop_size):
        raw[k] = swap(raw[2] if k == 3 else block_input_rows, "loop", 1 if k == 3 else k)

    length = -(-(rows + (blocks + 1) * tiles) // 8) * 8
    *own_parts, packed, second, mod = call(
        own_rows,
        [
            *(2 * cut(OWN_PIECES, LANES)),
            ((length, LANES), f32),
            ((rank, features), bf16),
            ((8, features), f32),
        ],
        [],
        scratch=[
            pltpu.VMEM((features, hidden), bf16),
            pltpu.VMEM((rows, features), bf16),
            pltpu.VMEM((rows, features), bf16),
            pltpu.VMEM((3, modulation.shape[0], features), f32),
            dma((4 + OWN_PIECES,)),
        ],
        scalars=[timestep_index],
        remote=[
            block_input_rows,
            cotangent,
            jnp.transpose(modulation, (1, 0, 2)),
            down_second_factor,
            frozen_up_weight,
        ],
        grant=OWN_GRANT,
    )
    (packed,) = call(add_packed, [((length, LANES), f32)], [packed, swap(packed, "sub", 1)])
    low_back, table = call(
        unpack,
        [((rows, LANES), bf16), ((-(-(blocks + 1) // 8) * 8, hidden), f32)],
        list(exchange(packed, "narrow", f32)),
    )
    pairs = []
    activated = []
    received = []

    def cores(parts):
        count = len(parts) // 2
        return parts[:count] + swap_all(parts[count:])

    def multiply(place, after):
        return call(
            up_rows, 2 * cut(UP_PIECES[min(place, 2)], LANES), [raw[order[place]], mod, frozen_up_weight], after
        )

    def add(parts, after):
        (value,) = call(add_cores, [((middle, hidden + LANES), bf16)], cores(parts), after)
        pairs.append(exchange(value, "narrow", bf16))
        return [value]

    def activate(after):
        place = len(activated)
        parts = call(
            named(gelu_rows, features),
            cut(GELU_PIECES),
            [*pairs[place], table],
            after,
        )
        activated.append([*parts, *swap_all(parts)])
        return parts[:1]

    def down(place, after):
        operands = [frozen_down_weight, first, low_back, *activated[place]]
        (joined,) = call(down_rows, [((rows, wide), bf16)], operands, after)
        received.append(swap(joined, "loop", order[place]))
        return [joined]

    def wait(after):
        return call(touch, [((8, LANES), f32)], [], after)

    last = len(order)
    after = [packed]
    for place in range(last):
        if place >= 2:
            after = activate(after)
        parts = multiply(place, after)
        after = parts[:1]
        if place == 0:
            after = after + [table]
        if place >= 2:
            after = down(place - 2, after)
        after = add(parts, after)
        if place == OWN_PLACE:
            after = add(own_parts, after)
            own_pair = pairs.pop()
    after = activate(after)
    after = wait(after + received[-1:])
    if OWN_PLACE > 2:
        after = add(own_parts, after)
        own_pair = pairs.pop()
    else:
        for _ in range(TOUCHES):
            after = wait(after)
    after = down(last - 2, after)
    after = activate(after)
    after = wait(down(last - 1, after) + received[-2:-1])
    pairs.append(own_pair)
    after = activate(after)
    own = activated[last]
    *contribution, low_total = call(
        named(second_gradient_part, last),
        [*(2 * [((rank // 2, features), bf16)]), ((rows, rank), f32)],
        [first, cotangent, mod, *received, *own],
        after,
        scratch=[pltpu.VMEM((rows, rank), f32)],
    )
    (block_update,) = call(
        named(update_rows, last),
        [((rows, features), bf16)],
        [frozen_down_weight, low_total, second, mod, *received, *own],
        scratch=[pltpu.VMEM((rows, features), f32)],
    )
    gathered = []
    for parts, rows_of in zip(activated, received + [low_back]):
        gathered += [*parts, rows_of]
    first_gradient, done = call(
        named(first_gradient_rows, len(cut(GELU_PIECES))),
        [((rank, hidden), f32), ((8, LANES), f32)],
        gathered,
        [low_total],
    )
    if loop_size == 4:
        operands, after = [], [done]
        for half in contribution:
            after = call(add_pair, [(half.shape, bf16)], [half, swap(half, "loop", 1)], after)
            operands += [after[0], swap(after[0], "loop", 2)]
        (second_gradient,) = call(add_halves, [((rank, features), f32)], operands)
    else:
        halves = [lax.psum(half, "loop") for half in contribution]
        second_gradient = jnp.concatenate(halves, axis=0).astype(f32)
    return (block_update, first_gradient.T, second_gradient)


def solution(mesh):
    in_specs = (
        P(("groups", "loop"), ("narrow", "sub")),
        P(("narrow", "sub"), "loop"),
        P("loop", ("narrow", "sub")),
        P(),
        P(),
        P(None, None, ("narrow", "sub")),
        P("groups"),
        P(("groups", "loop"), ("narrow", "sub")),
    )
    out_specs = (
        P(("groups", "loop"), ("narrow", "sub")),
        P(("groups", "loop"), None),
        P("groups", ("narrow", "sub")),
    )
    return jax.shard_map(
        per_device, mesh=mesh, in_specs=in_specs, out_specs=out_specs, check_vma=False
    )
```

```python
import functools

import jax
import jax.numpy as jnp
from jax import lax
from jax.experimental import pallas as pl
from jax.experimental.pallas import tpu as pltpu
from jax.sharding import PartitionSpec as P

adapter_scale = 0.5
norm_eps = 1e-06
gelu_coef = 0.7978845608028654
f32 = jnp.float32
bf16 = jnp.bfloat16
LANES = 128
TOUCHES = 2
ORDER = [2, 3, 1]
OWN_PIECES = 3
UP_PIECES = (4, 2, 3)
OWN_PLACE = 0
GELU_PIECES = (4, 2, 2, 2)
OWN_GRANT = (64 * 1024 - 11440) * 1024


def gelu_value(pre_value):
    inner_arg = gelu_coef * (pre_value + 0.044715 * pre_value * pre_value * pre_value)
    return 0.5 * pre_value * (1.0 + jnp.tanh(inner_arg))


def dot(left, right):
    return jnp.dot(left, right, preferred_element_type=f32)


def dot_transposed(left, right):
    return lax.dot_general(left, right, (((1,), (1,)), ((), ())), preferred_element_type=f32)


def dot_rows(left, right):
    return lax.dot_general(left, right, (((0,), (0,)), ((), ())), preferred_element_type=f32)


def split_dot(product, left, right):
    high = left.astype(bf16)
    low = (left - high.astype(f32)).astype(bf16)
    return product(high, right) + product(low, right)


def swap(value, axis, distance):
    size = lax.axis_size(axis)
    return lax.ppermute(value, axis, [(i, i ^ distance) for i in range(size)])


def exchange(value, axis, kind):
    distance, size = 1, lax.axis_size(axis)
    while True:
        other = swap(value, axis, distance)
        distance *= 2
        if distance >= size:
            return value, other
        value = (value.astype(f32) + other.astype(f32)).astype(kind)


def call(body, outs, arrays, after=(), scratch=(), remote=(), scalars=(), grant=24 * 2**20):
    vmem = pl.BlockSpec(memory_space=pltpu.VMEM)
    specs = [pl.BlockSpec(memory_space=pltpu.SMEM)] * len(scalars)
    specs += [pl.BlockSpec(memory_space=pltpu.HBM)] * len(remote) + [vmem] * len(arrays)
    count = len(specs)
    specs += [pl.BlockSpec(memory_space=pl.ANY)] * len(after)
    total = len(specs)

    def kernel(*refs):
        body(*refs[:count], *refs[total:])

    results = pl.pallas_call(
        kernel,
        out_shape=[jax.ShapeDtypeStruct(shape, kind) for shape, kind in outs],
        in_specs=specs,
        out_specs=[vmem] * len(outs),
        scratch_shapes=list(scratch),
        compiler_params=pltpu.CompilerParams(vmem_limit_bytes=grant),
        cost_estimate=pl.CostEstimate(flops=1024, bytes_accessed=1024, transcendentals=0),
        name=body.__name__,
    )(*scalars, *remote, *arrays, *after)
    return list(results)


def pieces(width, count):
    tiles = width // LANES
    count = min(count, tiles)
    return [(tiles * (k + 1) // count - tiles * k // count) * LANES for k in range(count)]


def bases(arrays):
    at = 0
    for array in arrays:
        yield array, at
        at += array.shape[1]


def unit_pieces(arrays):
    for place, (array, base) in enumerate(bases(arrays)):
        yield array, base, array.shape[1] - (LANES if place == len(arrays) - 1 else 0)


def columns(width, step=512):
    return [slice(at, min(at + step, width)) for at in range(0, width, step)]


def rows_at(place, count):
    return pl.ds(pl.multiple_of(place * count, count), count)


def own_core():
    return lax.axis_index("sub")


def feature_block():
    return lax.axis_index("narrow") * lax.axis_size("sub") + lax.axis_index("sub")


def centred(x, mod):
    values = x[...].astype(f32)
    total = jnp.sum(values, axis=1, keepdims=True)
    rows = (values - total / x.shape[1]) * (1.0 + mod[1:2, :])
    return rows.astype(bf16), total, values


def three_terms(value):
    high = value.astype(bf16).astype(f32)
    middle = (value - high).astype(bf16).astype(f32)
    return [high, middle, value - high - middle]


def sum_lanes(values, total):
    squares = jnp.sum(values * values, axis=1, keepdims=True)
    lane = lax.broadcasted_iota(jnp.int32, (values.shape[0], LANES), 1) - 8 * feature_block()
    lanes = jnp.zeros((values.shape[0], LANES), f32)
    for place, term in enumerate(three_terms(total) + three_terms(squares)):
        lanes = jnp.where(lane == place, term, lanes)
    return lanes.astype(bf16)


def split_rows(value):
    high = value.astype(bf16)
    return [high, (value - high.astype(f32)).astype(bf16)]


def order_rows(value):
    middle = value.shape[0] // 2
    low, high = value[:middle], value[middle:]
    own = own_core()
    return [jnp.where(own == 0, low, high), jnp.where(own == 0, high, low)]


def own_rows(step, x_hbm, cot_hbm, mod_hbm, second_hbm, weight_hbm, *refs):
    *parts, packed, factor, mod, weight, x, cot, table, sems = refs
    kept, sent = parts[: len(parts) // 2], parts[len(parts) // 2 :]
    rows, features = x.shape
    rank = factor.shape[0]
    hidden = weight.shape[1]
    tiles = hidden // LANES
    block = feature_block()
    blocks = lax.axis_size("narrow") * lax.axis_size("sub")
    at = pl.ds(pl.multiple_of(block * features, LANES), features)
    copies = [
        pltpu.make_async_copy(mod_hbm, table, sems.at[0]),
        pltpu.make_async_copy(x_hbm, x, sems.at[1]),
        pltpu.make_async_copy(cot_hbm, cot, sems.at[2]),
        pltpu.make_async_copy(second_hbm.at[:, at], factor, sems.at[3]),
    ]
    loads = []
    for _, base, width in unit_pieces(kept):
        at = slice(base, base + width)
        loads.append(pltpu.make_async_copy(weight_hbm.at[:, at], weight.at[:, at], sems.at[4 + len(loads)]))
    for copy in copies + loads:
        copy.start()
    copies[0].wait()
    for kind in range(3):
        mod[kind : kind + 1, :] = table[kind, pl.ds(step[0], 1), :]
    copies[1].wait()
    normed, total, values = centred(x, mod)
    lanes = jnp.concatenate(order_rows(sum_lanes(values, total)), axis=0)
    extra = split_rows(1.0 + mod[1:2, :]) + split_rows(mod[0:1, :])
    extra.append(jnp.zeros((16 - len(extra), features), bf16))
    left_rows = jnp.concatenate(order_rows(normed) + extra, axis=0)
    for copy in copies[2:]:
        copy.wait()
    back_rows = (mod[2:3, :] * cot[...].astype(f32)).astype(bf16)
    padded = jnp.concatenate([jnp.zeros((LANES - rank, features), bf16), factor[...]], axis=0)
    packed[:rows] = dot_transposed(back_rows, padded)
    packed[rows:] = jnp.zeros((packed.shape[0] - rows, LANES), f32)
    middle = rows // 2
    kept[-1][:, -LANES:] = lanes[:middle]
    sent[-1][:, -LANES:] = lanes[middle:]
    for (piece, base, width), other, load in zip(unit_pieces(kept), sent, loads):
        load.wait()
        for at in columns(width):
            product = dot(left_rows, weight[:, base + at.start : base + at.stop])
            piece[:, at] = product[:middle].astype(bf16)
            other[:, at] = product[middle:rows].astype(bf16)
            scale_row = product[rows : rows + 1] + product[rows + 1 : rows + 2]
            shift_row = product[rows + 2 : rows + 3] + product[rows + 3 : rows + 4]
            for tile in range((at.stop - at.start) // LANES):
                lanes = slice(tile * LANES, (tile + 1) * LANES)
                place = rows + (base + at.start) // LANES + tile
                packed[pl.ds(place + block * tiles, 1), :] = scale_row[:, lanes]
                packed[place + blocks * tiles : place + blocks * tiles + 1, :] = shift_row[:, lanes]


def add_packed(left, right, out):
    out[...] = left[...] + right[...]


def unpack(left, right, low_back, table):
    rows, tiles = low_back.shape[0], table.shape[1] // LANES
    low_back[...] = (left[:rows] + right[:rows]).astype(bf16)
    count = (left.shape[0] - rows) // tiles
    for kind in range(count):
        for tile in range(tiles):
            at = slice(rows + kind * tiles + tile, rows + kind * tiles + tile + 1)
            table[kind : kind + 1, tile * LANES : (tile + 1) * LANES] = left[at] + right[at]


def up_rows(x, mod, weight, *parts):
    kept, sent = parts[: len(parts) // 2], parts[len(parts) // 2 :]
    middle = x.shape[0] // 2
    normed, total, values = centred(x, mod)
    rows = jnp.concatenate(order_rows(normed), axis=0)
    lanes = jnp.concatenate(order_rows(sum_lanes(values, total)), axis=0)
    kept[-1][:, -LANES:] = lanes[:middle]
    sent[-1][:, -LANES:] = lanes[middle:]
    for (piece, base, width), other in zip(unit_pieces(kept), sent):
        for at in columns(width):
            product = dot(rows, weight[:, base + at.start : base + at.stop]).astype(bf16)
            piece[:, at] = product[:middle]
            other[:, at] = product[middle:]


def add_cores(*refs):
    *parts, out = refs
    kept, received = parts[: len(parts) // 2], parts[len(parts) // 2 :]
    for (piece, base), other in zip(bases(kept), received):
        total = piece[...].astype(f32) + other[...].astype(f32)
        out[:, base : base + piece.shape[1]] = total.astype(bf16)


def touch(out):
    out[...] = jnp.zeros_like(out)


def gelu_rows(features, mine, other, table, *parts):
    blocks = lax.axis_size("narrow") * lax.axis_size("sub")
    lanes = mine[:, -LANES:].astype(f32) + other[:, -LANES:].astype(f32)

    def term(place):
        return lanes[:, place : place + 1] + lanes[:, place + 1 : place + 2] + lanes[:, place + 2 : place + 3]

    sums = [term(8 * block) for block in range(blocks)]
    squares = [term(8 * block + 3) for block in range(blocks)]
    row_mean = sum(sums[1:], sums[0]) / (blocks * features)
    row_msq = sum(squares[1:], squares[0]) / (blocks * features)
    inv_std = lax.rsqrt(row_msq - row_mean * row_mean + norm_eps)
    offsets = [value / features - row_mean for value in sums]
    for out, start in bases(parts):
        for at in columns(out.shape[1]):
            source = slice(at.start + start, at.stop + start)
            value = mine[:, source].astype(f32) + other[:, source].astype(f32)
            for block in range(blocks):
                value = value + offsets[block] * table[block : block + 1, source]
            pre_act = inv_std * value + table[blocks : blocks + 1, source]
            out[:, at] = gelu_value(pre_act).astype(bf16)


def both_cores(parts):
    count = len(parts) // 2
    return [jnp.concatenate([a[...], b[...]], axis=0) for a, b in zip(parts[:count], parts[count:])]


def low_product(activated, first):
    hidden = sum(piece.shape[1] for piece in activated)
    place = lax.axis_index("loop") * hidden
    terms = []
    for piece, base in bases(activated):
        at = pl.ds(pl.multiple_of(place + base, LANES), piece.shape[1])
        terms.append(dot_transposed(piece, first[:, at]))
    return sum(terms[1:], terms[0])


def down_product(activated, weight, at):
    terms = [dot(piece, weight[base : base + piece.shape[1], at]) for piece, base in bases(activated)]
    return sum(terms[1:], terms[0])


def store_rows(out, at, value):
    middle = value.shape[0] // 2
    own = own_core()
    out[rows_at(own, middle), at] = value[:middle].astype(out.dtype)
    out[rows_at(1 - own, middle), at] = value[middle:].astype(out.dtype)


def down_rows(weight, first, low_back, *refs):
    *parts, out = refs
    activated = both_cores(parts)
    features = weight.shape[1]
    low = low_product(activated, first)
    low = jnp.concatenate([low, jnp.zeros((low.shape[0], LANES - low.shape[1]), f32)], axis=1)
    last = slice(features, features + LANES)
    store_rows(out, last, low)
    out[:, last] = (out[:, last].astype(f32) + low_back[...].astype(f32)).astype(bf16)
    for at in columns(features, 256):
        store_rows(out, at, down_product(activated, weight, at))


def columns_of(parts, at):
    for piece, base in bases(parts):
        if base <= at.start < base + piece.shape[1]:
            return piece[:, at.start - base : at.stop - base]


def first_gradient_rows(counts, *refs):
    *arrays, out, done = refs
    done[...] = jnp.zeros_like(done)
    rank, hidden = out.shape
    own = own_core()
    factors, mine, other = [], [], []
    for count in counts:
        block, arrays = arrays[: 2 * count + 1], arrays[2 * count + 1 :]
        middle = block[0].shape[0]
        factors += [block[-1][rows_at(core, middle), -LANES:] for core in (own, 1 - own)]
        mine.append(block[:count])
        other.append(block[count : 2 * count])
    factors = jnp.concatenate(factors, axis=0)
    for at in columns(hidden, 256 if hidden % 1536 == 0 else LANES):
        right = []
        for parts in zip(mine, other):
            right += [columns_of(piece, at) for piece in parts]
        product = dot_rows(factors, jnp.concatenate(right, axis=0))
        out[:, at] = adapter_scale * product[LANES - rank :]


def second_gradient_part(terms, first, cot, mod, *refs):
    *arrays, upper, lower, low_total, low = refs
    received, parts = arrays[:terms], arrays[terms:]
    rank, features = first.shape[0], cot.shape[1]
    back_rows = (mod[2:3, :] * cot[...].astype(f32)).astype(bf16)
    store_rows(low, slice(0, rank), low_product(both_cores(parts), first))
    sums = low[...]
    for value in received:
        sums = sums + value[:, features : features + rank].astype(f32)
    low_total[...] = sums
    product = (adapter_scale * split_dot(dot_rows, sums, back_rows)).astype(bf16)
    upper[...] = product[: rank // 2]
    lower[...] = product[rank // 2 :]


def update_rows(terms, weight, low_total, factor, mod, *refs):
    *arrays, out, total = refs
    received, parts = arrays[:terms], arrays[terms:]
    activated = both_cores(parts)
    features = factor.shape[1]
    for at in columns(features, 256):
        store_rows(total, at, down_product(activated, weight, at))
    base = total[...] + adapter_scale * split_dot(dot, low_total[...], factor[...])
    for value in received:
        base = base + value[:, :features].astype(f32)
    out[...] = (mod[2:3, :] * base).astype(bf16)


def add_pair(left, right, out):
    out[...] = (left[...].astype(f32) + right[...].astype(f32)).astype(out.dtype)


def add_halves(upper, upper_other, lower, lower_other, out):
    middle = upper.shape[0]
    out[:middle] = upper[...].astype(f32) + upper_other[...].astype(f32)
    out[middle:] = lower[...].astype(f32) + lower_other[...].astype(f32)


def per_device(
    block_input_rows,
    frozen_up_weight,
    frozen_down_weight,
    down_first_factor,
    down_second_factor,
    modulation,
    timestep_index,
    cotangent,
):
    loop_size = lax.axis_size("loop")
    wide_size = lax.axis_size("narrow") * lax.axis_size("sub")
    rows, features = block_input_rows.shape
    hidden = frozen_up_weight.shape[1]
    rank = down_first_factor.shape[1]
    blocks = wide_size
    middle = rows // 2
    wide = features + LANES
    first = down_first_factor.T
    tiles = hidden // LANES
    dma = pltpu.SemaphoreType.DMA

    def swap_all(parts):
        return [swap(part, "sub", 1) for part in parts]

    def cut(count, extra=0):
        widths = pieces(hidden, count)
        widths[-1] += extra
        return [((middle, width), bf16) for width in widths]

    def named(body, *values):
        bound = functools.partial(body, *values)
        bound.__name__ = body.__name__
        return bound

    order = ORDER if loop_size == 4 else list(range(1, loop_size))
    raw = {k: swap(block_input_rows, "loop", k) for k in range(1, min(loop_size, 3))}
    for k in range(3, loop_size):
        raw[k] = swap(raw[2] if k == 3 else block_input_rows, "loop", 1 if k == 3 else k)

    length = -(-(rows + (blocks + 1) * tiles) // 8) * 8
    *own_parts, packed, second, mod = call(
        own_rows,
        [
            *(2 * cut(OWN_PIECES, LANES)),
            ((length, LANES), f32),
            ((rank, features), bf16),
            ((8, features), f32),
        ],
        [],
        scratch=[
            pltpu.VMEM((features, hidden), bf16),
            pltpu.VMEM((rows, features), bf16),
            pltpu.VMEM((rows, features), bf16),
            pltpu.VMEM((3, modulation.shape[0], features), f32),
            dma((4 + OWN_PIECES,)),
        ],
        scalars=[timestep_index],
        remote=[
            block_input_rows,
            cotangent,
            jnp.transpose(modulation, (1, 0, 2)),
            down_second_factor,
            frozen_up_weight,
        ],
        grant=OWN_GRANT,
    )
    (packed,) = call(add_packed, [((length, LANES), f32)], [packed, swap(packed, "sub", 1)])
    low_back, table = call(
        unpack,
        [((rows, LANES), bf16), ((-(-(blocks + 1) // 8) * 8, hidden), f32)],
        list(exchange(packed, "narrow", f32)),
    )
    pairs = []
    activated = []
    received = []

    def cores(parts):
        count = len(parts) // 2
        return parts[:count] + swap_all(parts[count:])

    def multiply(place, after):
        return call(
            up_rows, 2 * cut(UP_PIECES[min(place, 2)], LANES), [raw[order[place]], mod, frozen_up_weight], after
        )

    def add(parts, after):
        (value,) = call(add_cores, [((middle, hidden + LANES), bf16)], cores(parts), after)
        pairs.append(exchange(value, "narrow", bf16))
        return [value]

    def activate(after):
        place = len(activated)
        parts = call(
            named(gelu_rows, features),
            cut(GELU_PIECES[min(place, 3)]),
            [*pairs[place], table],
            after,
        )
        activated.append([*parts, *swap_all(parts)])
        return parts[:1]

    def down(place, after):
        operands = [frozen_down_weight, first, low_back, *activated[place]]
        (joined,) = call(down_rows, [((rows, wide), bf16)], operands, after)
        received.append(swap(joined, "loop", order[place]))
        return [joined]

    def wait(after):
        return call(touch, [((8, LANES), f32)], [], after)

    last = len(order)
    after = [packed]
    for place in range(last):
        if place >= 2:
            after = activate(after)
        parts = multiply(place, after)
        after = parts[:1]
        if place == 0:
            after = after + [table]
        if place >= 2:
            after = down(place - 2, after)
        after = add(parts, after)
        if place == OWN_PLACE:
            after = add(own_parts, after)
            own_pair = pairs.pop()
    after = activate(after)
    after = wait(after + received[-1:])
    if OWN_PLACE > 2:
        after = add(own_parts, after)
        own_pair = pairs.pop()
    else:
        for _ in range(TOUCHES):
            after = wait(after)
    after = down(last - 2, after)
    after = activate(after)
    after = wait(down(last - 1, after) + received[-2:-1])
    pairs.append(own_pair)
    after = activate(after)
    own = activated[last]
    *contribution, low_total = call(
        named(second_gradient_part, last),
        [*(2 * [((rank // 2, features), bf16)]), ((rows, rank), f32)],
        [first, cotangent, mod, *received, *own],
        after,
        scratch=[pltpu.VMEM((rows, rank), f32)],
    )
    (block_update,) = call(
        named(update_rows, last),
        [((rows, features), bf16)],
        [frozen_down_weight, low_total, second, mod, *received, *own],
        scratch=[pltpu.VMEM((rows, features), f32)],
    )
    gathered = []
    for parts, rows_of in zip(activated, received + [low_back]):
        gathered += [*parts, rows_of]
    first_gradient, done = call(
        named(first_gradient_rows, [len(parts) // 2 for parts in activated]),
        [((rank, hidden), f32), ((8, LANES), f32)],
        gathered,
        [low_total],
    )
    if loop_size == 4:
        operands, after = [], [done]
        for half in contribution:
            after = call(add_pair, [(half.shape, bf16)], [half, swap(half, "loop", 1)], after)
            operands += [after[0], swap(after[0], "loop", 2)]
        (second_gradient,) = call(add_halves, [((rank, features), f32)], operands)
    else:
        halves = [lax.psum(half, "loop") for half in contribution]
        second_gradient = jnp.concatenate(halves, axis=0).astype(f32)
    return (block_update, first_gradient.T, second_gradient)


def solution(mesh):
    in_specs = (
        P(("groups", "loop"), ("narrow", "sub")),
        P(("narrow", "sub"), "loop"),
        P("loop", ("narrow", "sub")),
        P(),
        P(),
        P(None, None, ("narrow", "sub")),
        P("groups"),
        P(("groups", "loop"), ("narrow", "sub")),
    )
    out_specs = (
        P(("groups", "loop"), ("narrow", "sub")),
        P(("groups", "loop"), None),
        P("groups", ("narrow", "sub")),
    )
    return jax.shard_map(
        per_device, mesh=mesh, in_specs=in_specs, out_specs=out_specs, check_vma=False
    )
```
